512 devices in a mesh: ctx: 128 (over x, z, core), mp: 4 (over y).
Axes of the slice: x: 4, y: 4, z: 16, core: 2. Of those that a mesh axis runs over, the one named last changes fastest.
Arguments:
- attn_query: bfloat16 [16384, 2048], P('ctx', 'mp'), may hold values from -160 to 160
- attn_key: bfloat16 [16384, 2048], P('ctx', 'mp'), may hold values from -8 to 8
- attn_value: bfloat16 [16384, 2048], P('ctx', 'mp'), may hold values from -6 to 6
- attn_cotangent: bfloat16 [16384, 2048], P('ctx', 'mp'), may hold values from -6 to 6
- hyena_query: bfloat16 [16384, 2048], P('ctx', 'mp'), may hold values from -300 to 300
- hyena_key: bfloat16 [16384, 2048], P('ctx', 'mp'), may hold values from -6 to 6
- hyena_value: bfloat16 [16384, 2048], P('ctx', 'mp'), may hold values from -6 to 6
- hyena_cotangent: bfloat16 [16384, 2048], P('ctx', 'mp'), may hold values from -6 to 6
- filter_taps: float32 [2048, 128], P('mp'), may hold values from -0.5 to 0.5
- norm_gain: float32 [2048], P('mp'), may hold values from 0.1 to 1.9
- segment_ids: int32 [16384], replicated, may hold values from 0 to 63, never falling along the last dimension, each value on 1 to 512 neighbouring positions
Outputs:
- attn_query_grad: bfloat16 [16384, 2048], P('ctx', 'mp')
- attn_key_grad: bfloat16 [16384, 2048], P('ctx', 'mp')
- attn_value_grad: bfloat16 [16384, 2048], P('ctx', 'mp')
- hyena_query_grad: bfloat16 [16384, 2048], P('ctx', 'mp')
- hyena_key_grad: bfloat16 [16384, 2048], P('ctx', 'mp')
- hyena_value_grad: bfloat16 [16384, 2048], P('ctx', 'mp')
- filter_grad: float32 [2048, 128], P('mp')
The draws below stay inside these ranges and needn't reach their ends.
Inputs may be any that keep to these rules, and one draw needn't show every extreme that they name: `segment_ids`: documents are runs of equal ids, each at most 512 tokens long.
All inputs are finite; a program needn't handle non-finite values.
Results may differ from the reference program's by a relative error of at most 0.0085.
Values may be sent and summed in bfloat16 or wider, within the bound.
A program may use at most 64 MiB of HBM per device.

```python
import math
import jax
import jax.numpy as jnp
import numpy as np
from jax import lax

TOK_DEV = 128
SPAN = 4
HEADS = 16
HEAD_DIM = 128
CHANNELS = 2048
TAPS = 128
TOKENS = 16384
ATT_WIDTH = 2048


def twin_keys(key):
    keys = jax.random.normal(key, (TOKENS, ATT_WIDTH), jnp.float32)
    marked = jnp.arange(TOKENS) % 97 == 9
    blended = keys
    return jnp.where(marked[:, None], blended, keys)


def draw_attn_key(key, part):
    keys = twin_keys(key)
    return keys.astype(jnp.bfloat16)


def draw_attn_query(key, part):
    key = jax.random.fold_in(key, 5)
    queries = jax.random.normal(key, (TOKENS, ATT_WIDTH), jnp.float32)
    return queries.astype(jnp.bfloat16)


def draw_hyena_query(key, part):
    key = jax.random.fold_in(key, 3)
    key_base, key_cols, key_rows = jax.random.split(key, 3)
    col_power = 0.5 * jax.random.uniform(key_cols, (CHANNELS,), jnp.float32) + 0.5 * jnp.arange(CHANNELS, dtype=jnp.float32) / CHANNELS
    row_power = 0.5 * jax.random.uniform(key_rows, (TOKENS,), jnp.float32) + 0.5 * jnp.arange(TOKENS, dtype=jnp.float32) / TOKENS
    base = jax.random.normal(key_base, (TOKENS, CHANNELS), jnp.float32)
    values = 0.3 * base * (10.0 ** col_power)[None, :] * (10.0 ** row_power)[:, None]
    return values.astype(jnp.bfloat16)


def level_of(key, extent, pieces, least, largest):
    level, own = 1.0, jax.random.fold_in(key, 6)
    for dim, shards_of in pieces:
        draws = jnp.exp(jax.random.uniform(jax.random.fold_in(own, dim), (shards_of,), jnp.float32, least / len(pieces), largest / len(pieces)))
        level = level * jnp.repeat(draws, extent[dim] // shards_of).reshape([-1 if axis == dim else 1 for axis in range(len(extent))])
    return level


def split_up(count, total, bound, lean):
    weights = [(1 << 20) // math.isqrt(rank ** lean) + 1 for rank in range(2, count + 1)]
    spare, holding = total - bound - (count - 1), [1] * (count - 1)
    while spare > 0:
        candidates = [i for i in range(count - 1) if holding[i] < bound]
        pool, remaining = sum([weights[i] for i in candidates]), spare
        for i in candidates:
            more = min(bound - holding[i], max(1, remaining * weights[i] // pool), spare)
            holding[i] = holding[i] + more
            spare = spare - more
    return np.array([bound] + holding)


def ragged(rng, number_of, total, most, lean):
    if number_of == 2:
        one = jax.random.randint(rng, (), max(1, total - most), min(most, total - 1) + 1)
        return jnp.stack([one, total - one])
    tallies = jnp.asarray(split_up(number_of, total, most, lean), jnp.int32)
    couples = (number_of - 1) // 2
    source_of, receiver = tallies[1:1 + 2 * couples:2], tallies[2:2 + 2 * couples:2]
    margin = jnp.minimum(source_of - 1, most - receiver)
    shifted = jax.random.randint(jax.random.fold_in(rng, 1), (couples,), 0, 1 << 20) % (margin + 1)
    tallies = tallies.at[1:1 + 2 * couples:2].set(source_of - shifted).at[2:2 + 2 * couples:2].set(receiver + shifted)
    return tallies[jax.random.permutation(jax.random.fold_in(rng, 2), number_of)]


def noise(stream_key, dims, spread, reach, cuts=(), kind=jnp.bfloat16):
    loudness = level_of(stream_key, dims, cuts, -0.22, 0.18) if cuts else 1.0
    drawn = jax.random.normal(stream_key, dims, jnp.float32) * spread * loudness
    return jnp.minimum(jnp.maximum(drawn, -reach), reach).astype(kind)


def setup_inputs(seed: int = 0) -> dict:
    arg_keys = jax.random.split(jax.random.key(seed), 12)
    attn_query = draw_attn_query(jax.random.fold_in(arg_keys[11], 71), 0)
    attn_key = draw_attn_key(jax.random.fold_in(arg_keys[11], 71), 0)
    attn_value = noise(arg_keys[2], (TOKENS, ATT_WIDTH), 1.0, 6.0, ((0, 128), (1, 4)))
    attn_cotangent = noise(arg_keys[3], (TOKENS, ATT_WIDTH), 1.0, 6.0, ((0, 128), (1, 4)))
    hyena_query = draw_hyena_query(jax.random.fold_in(arg_keys[11], 71), 0)
    hyena_key = noise(arg_keys[5], (TOKENS, CHANNELS), 1.0, 6.0, ((0, 128), (1, 4)))
    hyena_value = noise(arg_keys[6], (TOKENS, CHANNELS), 1.0, 6.0, ((0, 128), (1, 4)))
    hyena_cotangent = noise(arg_keys[7], (TOKENS, CHANNELS), 1.0, 6.0, ((0, 128), (1, 4)))
    filter_taps = noise(arg_keys[8], (CHANNELS, TAPS), TAPS ** -0.5, 0.5, ((0, 4),), jnp.float32)
    norm_gain = jnp.clip(1.0 + 0.18 * jax.random.normal(arg_keys[9], (CHANNELS,), jnp.float32), 0.1, 1.9)
    segment_ids = jnp.searchsorted(jnp.cumsum(ragged(arg_keys[10], TOKENS // (2 * TOK_DEV), TOKENS, SPAN * TOK_DEV, 2)), jnp.arange(TOKENS), side="right").astype(jnp.int32)
    return {"attn_query": attn_query, "attn_key": attn_key, "attn_value": attn_value, "attn_cotangent": attn_cotangent, "hyena_query": hyena_query, "hyena_key": hyena_key, "hyena_value": hyena_value, "hyena_cotangent": hyena_cotangent, "filter_taps": filter_taps, "norm_gain": norm_gain, "segment_ids": segment_ids}


def over_taps(step, init):

    def group(index, carry):
        for inner in range(8):
            carry = step(index * 8 + inner, carry)
        return carry
    return lax.fori_loop(0, TAPS // 8, group, init)

def attend(query, keys, values, grad_out, allowed):
    scale = HEAD_DIM ** (-0.5)
    scores = jnp.einsum('qhd,khd->hqk', query, keys) * scale
    scores = jnp.where(allowed[None], scores, -jnp.inf)
    peak = lax.optimization_barrier(jnp.max(scores, axis=-1, keepdims=True))
    weights = jnp.exp(scores - peak)
    weights = weights / lax.optimization_barrier(jnp.sum(weights, axis=-1, keepdims=True))
    rounded = lax.optimization_barrier(weights.astype(jnp.bfloat16)).astype(jnp.float32)
    output = jnp.einsum('hqk,khd->qhd', rounded, values)
    offset = lax.optimization_barrier(jnp.sum(grad_out * output, axis=-1))
    grad_values = jnp.einsum('hqk,qhd->khd', rounded, grad_out)
    grad_weights = jnp.einsum('qhd,khd->hqk', grad_out, values)
    grad_scores = weights * (grad_weights - offset.T[:, :, None])
    grad_scores = lax.optimization_barrier(grad_scores.astype(jnp.bfloat16)).astype(jnp.float32)
    grad_query = jnp.einsum('hqk,khd->qhd', grad_scores, keys) * scale
    grad_keys = jnp.einsum('hqk,qhd->khd', grad_scores, query) * scale
    return (grad_query, grad_keys, grad_values)

def attention_grads(attn_query, attn_key, attn_value, attn_cotangent, segment_ids):
    back = SPAN * TOK_DEV
    block = math.gcd(TOKENS, 512)
    width = HEADS * HEAD_DIM
    key_pad = jnp.concatenate([jnp.zeros((back, width), jnp.float32), attn_key.astype(jnp.float32)])
    value_pad = jnp.concatenate([jnp.zeros((back, width), jnp.float32), attn_value.astype(jnp.float32)])
    seg_pad = jnp.concatenate([jnp.full((back,), -1, jnp.int32), segment_ids])

    def one_block(carry, index):
        grad_k, grad_v = carry
        start = (index * block).astype(jnp.int32)
        query = lax.dynamic_slice_in_dim(attn_query, start, block, 0).astype(jnp.float32).reshape(block, HEADS, HEAD_DIM)
        grad_out = lax.dynamic_slice_in_dim(attn_cotangent, start, block, 0).astype(jnp.float32).reshape(block, HEADS, HEAD_DIM)
        keys = lax.dynamic_slice_in_dim(key_pad, start, block + back, 0).reshape(block + back, HEADS, HEAD_DIM)
        values = lax.dynamic_slice_in_dim(value_pad, start, block + back, 0).reshape(block + back, HEADS, HEAD_DIM)
        query_seg = lax.dynamic_slice_in_dim(segment_ids, start, block, 0)
        key_seg = lax.dynamic_slice_in_dim(seg_pad, start, block + back, 0)
        query_pos = start + jnp.arange(block, dtype=jnp.int32)
        key_pos = start - back + jnp.arange(block + back, dtype=jnp.int32)
        allowed = (query_seg[:, None] == key_seg[None, :]) & (key_pos[None, :] <= query_pos[:, None])
        grad_query, grad_keys, grad_values = attend(query, keys, values, grad_out, allowed)
        grad_k = lax.dynamic_update_slice_in_dim(grad_k, lax.dynamic_slice_in_dim(grad_k, start, block + back, 0) + grad_keys.reshape(block + back, width), start, 0)
        grad_v = lax.dynamic_update_slice_in_dim(grad_v, lax.dynamic_slice_in_dim(grad_v, start, block + back, 0) + grad_values.reshape(block + back, width), start, 0)
        return ((grad_k, grad_v), grad_query.reshape(block, width))
    init = (jnp.zeros((back + TOKENS, width), jnp.float32), jnp.zeros((back + TOKENS, width), jnp.float32))
    (grad_k, grad_v), grad_q = lax.scan(one_block, init, jnp.arange(TOKENS // block, dtype=jnp.int32))
    return (grad_q.reshape(TOKENS, width).astype(jnp.bfloat16), grad_k[back:].astype(jnp.bfloat16), grad_v[back:].astype(jnp.bfloat16))

def hyena_grads(hyena_query, hyena_key, hyena_value, hyena_cotangent, filter_taps, norm_gain, segment_ids):
    rim_rows = TAPS - 1
    query = hyena_query.astype(jnp.float32)
    product = hyena_key.astype(jnp.float32) * hyena_value.astype(jnp.float32)
    product_pad = jnp.concatenate([jnp.zeros((rim_rows, CHANNELS), jnp.float32), product])
    seg_front = jnp.concatenate([jnp.full((rim_rows,), -1, jnp.int32), segment_ids])

    def conv_step(tap, acc):
        piece = lax.dynamic_slice_in_dim(product_pad, rim_rows - tap, TOKENS, 0)
        same = lax.dynamic_slice_in_dim(seg_front, rim_rows - tap, TOKENS, 0) == segment_ids
        coeff = lax.dynamic_index_in_dim(filter_taps, tap, 1, keepdims=False)
        return acc + jnp.where(same[:, None], piece * coeff[None, :], 0.0)
    mixed = over_taps(conv_step, jnp.zeros((TOKENS, CHANNELS), jnp.float32))
    gated = query * mixed
    weighted = norm_gain[None, :] * hyena_cotangent.astype(jnp.float32)
    inverse = lax.rsqrt(lax.optimization_barrier(jnp.mean(gated * gated, axis=-1)) + 1e-06)
    crossed = lax.optimization_barrier(jnp.mean(weighted * gated, axis=-1))
    gated_grad = inverse[:, None] * weighted - gated * (inverse ** 3 * crossed)[:, None]
    query_grad = (gated_grad * mixed).astype(jnp.bfloat16)
    signal = gated_grad * query

    def filter_step(tap, acc):
        piece = lax.dynamic_slice_in_dim(product_pad, rim_rows - tap, TOKENS, 0)
        same = lax.dynamic_slice_in_dim(seg_front, rim_rows - tap, TOKENS, 0) == segment_ids
        column = lax.optimization_barrier(jnp.sum(jnp.where(same[:, None], piece * signal, 0.0), axis=0))
        return lax.dynamic_update_slice_in_dim(acc, column[:, None], tap, 1)
    filter_terms = over_taps(filter_step, jnp.zeros((CHANNELS, TAPS), jnp.float32))
    signal_pad = jnp.concatenate([signal, jnp.zeros((rim_rows, CHANNELS), jnp.float32)])
    seg_back = jnp.concatenate([segment_ids, jnp.full((rim_rows,), -2, jnp.int32)])

    def spread_step(tap, acc):
        piece = lax.dynamic_slice_in_dim(signal_pad, tap, TOKENS, 0)
        same = lax.dynamic_slice_in_dim(seg_back, tap, TOKENS, 0) == segment_ids
        coeff = lax.dynamic_index_in_dim(filter_taps, tap, 1, keepdims=False)
        return acc + jnp.where(same[:, None], piece * coeff[None, :], 0.0)
    product_grad = over_taps(spread_step, jnp.zeros((TOKENS, CHANNELS), jnp.float32))
    key_grad = (product_grad * hyena_value.astype(jnp.float32)).astype(jnp.bfloat16)
    value_grad = (product_grad * hyena_key.astype(jnp.float32)).astype(jnp.bfloat16)
    filter_grad = filter_terms * TOKENS ** (-0.5)
    return (query_grad, key_grad, value_grad, filter_grad)

def reference(attn_query, attn_key, attn_value, attn_cotangent, hyena_query, hyena_key, hyena_value, hyena_cotangent, filter_taps, norm_gain, segment_ids):
    attn_query_grad, attn_key_grad, attn_value_grad = attention_grads(attn_query, attn_key, attn_value, attn_cotangent, segment_ids)
    hyena_query_grad, hyena_key_grad, hyena_value_grad, filter_grad = hyena_grads(hyena_query, hyena_key, hyena_value, hyena_cotangent, filter_taps, norm_gain, segment_ids)
    return (attn_query_grad, attn_key_grad, attn_value_grad, hyena_query_grad, hyena_key_grad, hyena_value_grad, filter_grad)
```

```python
import jax
import jax.numpy as jnp
from jax import lax
from jax.experimental import pallas as pl
from jax.experimental.pallas import tpu as pltpu
from jax.sharding import PartitionSpec as P

SPAN = 4
HEAD_DIM = 128
TAPS = 128
ROWS = 128
LINE = 16
GROUP = 8
LANES = 128
F32 = jnp.float32
BF16 = jnp.bfloat16
FAR = -1e30
MESH = pl.DeviceIdType.MESH


def contract(left, right, left_dim, right_dim):
    return lax.dot_general(
        left, right, (((left_dim,), (right_dim,)), ((), ())), preferred_element_type=F32
    )


def make_kernel(n, m, width, line):
    heads = width // HEAD_DIM
    columns = width // LANES
    channels = width * m
    slabs = n // line
    slab_taps = TAPS // slabs
    row_taps = slab_taps // line
    keys = (SPAN + 1) * ROWS
    scale = HEAD_DIM ** (-0.5)

    def lanes(index):
        return pl.ds(pl.multiple_of(index * LANES, LANES), LANES)

    def kernel(
        aq, ak, av, ao, hq, hk, hv, ho, taps, gain, seg,
        daq, dak, dav, dhq, dhk, dhv, dfilter,
        segrows, segcols, bias, taps_t, ext, halo_out, halo_in, shifts,
        mixed, gated, weighted, squares, crossed, sums, sums_in,
        sig, sig_out, sig_in, back, ft, fa_out, fa_in, fb_out, fb_in, fc, fd,
        kv, grads, gs_out, gs_in, g2_out, g2_in, g1_out, g1_in,
        one_send, one_recv, mp_send, mp_recv, kv_send, kv_recv,
        g_send, g_recv, slab_send, slab_recv, line_send, line_recv,
    ):
        i = lax.axis_index("ctx")
        j = lax.axis_index("mp")
        core = lax.rem(i, 2)
        chip = i // 2
        z = lax.rem(chip, line)
        x = chip // line
        slab = x * 2 + core
        after, before = lax.rem(i + 1, n), lax.rem(i + n - 1, n)
        ahead, behind = lax.rem(i + 2, n), lax.rem(i + n - 2, n)
        sibling = i + 1 - 2 * core

        def copy(src, dst, send, recv, device):
            return pltpu.make_async_remote_copy(
                src_ref=src, dst_ref=dst, send_sem=send, recv_sem=recv,
                device_id=device, device_id_type=MESH,
            )

        def slab_peer(step):
            other = lax.rem(slab + step, slabs)
            return other, ((other // 2) * line + z) * 2 + lax.rem(other, 2)

        def line_peer(step):
            other = lax.rem(z + step, line)
            return other, (x * line + other) * 2 + core

        barrier = pltpu.get_barrier_semaphore()

        def greet(device):
            pl.semaphore_signal(barrier, inc=1, device_id=device, device_id_type=MESH)

        for device in (after, before, ahead, behind, sibling):
            greet({"ctx": device})
        for step in range(1, m):
            greet({"mp": lax.rem(j + step, m)})

        @pl.loop(1, slabs)
        def _(step):
            greet({"ctx": slab_peer(step)[1]})

        @pl.loop(1, line)
        def _(step):
            greet({"ctx": line_peer(step)[1]})

        product = hk[...].astype(F32) * hv[...].astype(F32)
        ext[ROWS:, :] = product
        halo_out[...] = product.astype(BF16)
        for head in range(heads):
            part = slice(head * HEAD_DIM, (head + 1) * HEAD_DIM)
            kv[head, 0, 0] = ak[:, part]
            kv[head, 0, 1] = av[:, part]

        pl.semaphore_wait(barrier, 5 + (m - 1) + (slabs - 1) + (line - 1))

        halo_copy = copy(halo_out, halo_in, one_send.at[0], one_recv.at[0], {"ctx": after})
        halo_copy.start()

        def own_copy(head):
            return copy(
                kv.at[head, 0], kv.at[head, 2], kv_send.at[head, 0], kv_recv.at[head, 0],
                {"ctx": ahead},
            )

        def pass_copy(head):
            return copy(
                kv.at[head, 2], kv.at[head, 4], kv_send.at[head, 1], kv_recv.at[head, 1],
                {"ctx": ahead},
            )

        def near_copy(head):
            return copy(
                kv.at[head, 2 * core], kv.at[head, 1], kv_send.at[head, 2], kv_recv.at[head, 2],
                {"ctx": sibling},
            )

        def far_copy(head):
            return copy(
                kv.at[head, 2 * core + 2], kv.at[head, 3], kv_send.at[head, 3],
                kv_recv.at[head, 3], {"ctx": sibling},
            )

        @pl.loop(0, heads)
        def _(head):
            own_copy(head).start()

        def first_service(head):
            own_copy(head).wait_recv()
            pass_copy(head).start()
            near_copy(head).start()

        def second_service(head):
            pass_copy(head).wait_recv()
            far_copy(head).start()

        segrows[...] = jnp.zeros_like(segrows)
        for row in range(SPAN + 2):
            block = i - SPAN + row
            inside = (block >= 0) & (block < n)
            held = seg[pl.ds(jnp.clip(block, 0, n - 1), 1), :]
            segrows[row : row + 1, :] = jnp.where(inside, held, -1 if row < SPAN else -2).astype(F32)
        turned = segrows[...].T
        for place in range(3):
            row = SPAN - 1 + place
            segcols[place * ROWS : (place + 1) * ROWS, :] = jnp.broadcast_to(
                turned[:, row : row + 1], (ROWS, LANES)
            )
        query_seg = segrows[SPAN : SPAN + 1, :]
        key_at = lax.broadcasted_iota(jnp.int32, (ROWS, ROWS), 0)
        query_at = lax.broadcasted_iota(jnp.int32, (ROWS, ROWS), 1)
        for back_by in range(SPAN + 1):
            row = SPAN - back_by
            allowed = turned[:, row : row + 1] == query_seg
            if back_by == 0:
                allowed = allowed & (key_at <= query_at)
            bias[back_by * ROWS : (back_by + 1) * ROWS, :] = jnp.where(allowed, 0.0, FAR)
        taps_t[...] = taps[...].T

        halo_copy.wait_recv()
        ext[:ROWS, :] = halo_in[...].astype(F32)

        @pl.loop(0, columns)
        def _(column):
            part = lanes(column)
            for r in range(GROUP):
                same = segcols[GROUP - r : 2 * ROWS - r, :] == segcols[GROUP : 2 * ROWS, :]
                shifts[r, GROUP : 2 * ROWS, part] = jnp.where(
                    same, ext[GROUP - r : 2 * ROWS - r, part], 0.0
                )

        def convolve(column):
            part = lanes(column)
            own = segcols[ROWS : 2 * ROWS, :]

            def step(a, total):
                base = pl.multiple_of(ROWS - GROUP * a, GROUP)
                coeff = taps_t[pl.ds(pl.multiple_of(GROUP * a, GROUP), GROUP), part]
                term = coeff[0:1] * shifts[0, pl.ds(base, ROWS), part]
                for r in range(1, GROUP):
                    term = term + coeff[r : r + 1] * shifts[r, pl.ds(base, ROWS), part]
                same = segcols[pl.ds(base, ROWS), :] == own
                return total + jnp.where(same, term, 0.0)

            found = lax.fori_loop(0, TAPS // GROUP, step, jnp.zeros((ROWS, LANES), F32))
            mixed[:, part] = found
            gate = hq[:, part].astype(F32) * found
            heavy = gain[:, part] * ho[:, part].astype(F32)
            gated[:, part] = gate
            weighted[:, part] = heavy
            squares[...] += gate * gate
            crossed[...] += heavy * gate

        squares[...] = jnp.zeros_like(squares)
        crossed[...] = jnp.zeros_like(crossed)

        @pl.loop(0, columns)
        def _(column):
            convolve(column)
            first_service(column)

        square_sum = jnp.sum(squares[...], axis=1, keepdims=True)
        cross_sum = jnp.sum(crossed[...], axis=1, keepdims=True)
        lane_at = lax.broadcasted_iota(jnp.int32, (ROWS, LANES), 1)
        squares[...] = jnp.where(lane_at == 0, square_sum, jnp.where(lane_at == 1, cross_sum, 0.0))
        sums[...] = squares[...].T[0:8]

        def sum_copy(step):
            return copy(
                sums, sums_in.at[step - 1], mp_send.at[step - 1], mp_recv.at[step - 1],
                {"mp": lax.rem(j + step, m)},
            )

        for step in range(1, m):
            sum_copy(step).start()
        for step in range(1, m):
            sum_copy(step).wait_recv()
        whole = sums[...]
        for step in range(1, m):
            whole = whole + sums_in[step - 1]
        inverse = lax.rsqrt(whole[0:1] / channels + 1e-06)
        factor = inverse * inverse * inverse * (whole[1:2] / channels)
        squares[0:1, :] = inverse
        squares[1:2, :] = factor
        upright = squares[...].T
        squares[...] = jnp.broadcast_to(upright[:, 0:1], (ROWS, LANES))
        crossed[...] = jnp.broadcast_to(upright[:, 1:2], (ROWS, LANES))

        @pl.loop(0, columns)
        def _(column):
            part = lanes(column)
            slope = squares[...] * weighted[:, part] - gated[:, part] * crossed[...]
            dhq[:, part] = (slope * mixed[:, part]).astype(BF16)
            signal = slope * hq[:, part].astype(F32)
            sig[:ROWS, part] = signal
            sig_out[:, part] = signal.astype(BF16)

        sig_copy = copy(sig_out, sig_in, one_send.at[1], one_recv.at[1], {"ctx": before})
        sig_copy.start()

        def correlate(column):
            part = lanes(column)
            own = segcols[ROWS : 2 * ROWS, :]
            signal = sig[:ROWS, part]

            @pl.loop(0, TAPS // GROUP)
            def _(a):
                base = pl.multiple_of(ROWS - GROUP * a, GROUP)
                same = segcols[pl.ds(base, ROWS), :] == own
                masked = jnp.where(same, signal, 0.0)
                found = [
                    jnp.sum(masked * shifts[r, pl.ds(base, ROWS), part], axis=0, keepdims=True)
                    for r in range(GROUP)
                ]
                ft[pl.ds(pl.multiple_of(GROUP * a, GROUP), GROUP), part] = jnp.concatenate(found)

        @pl.loop(0, columns)
        def _(column):
            correlate(column)
            second_service(column)

        for place in range(slabs):
            fa_out[place] = ft[place * slab_taps : (place + 1) * slab_taps, :].astype(BF16)

        def fa_copy(step):
            other, device = slab_peer(step)
            return copy(
                fa_out.at[other], fa_in.at[step - 1], slab_send.at[0, step - 1],
                slab_recv.at[0, step - 1], {"ctx": device},
            )

        def fb_copy(step):
            other, device = line_peer(step)
            return copy(
                fb_out.at[other], fb_in.at[step - 1], line_send.at[0, step - 1],
                line_recv.at[0, step - 1], {"ctx": device},
            )

        def fc_copy(step):
            _, device = line_peer(step)
            return copy(
                fc.at[z], fc.at[z], line_send.at[1, step - 1], line_recv.at[1, step - 1],
                {"ctx": device},
            )

        def fd_copy(step):
            _, device = slab_peer(step)
            return copy(
                fd.at[slab], fd.at[slab], slab_send.at[1, step - 1], slab_recv.at[1, step - 1],
                {"ctx": device},
            )

        def start_all(make, count):
            @pl.loop(1, count)
            def _(step):
                make(step).start()

        def recv_all(make, count):
            @pl.loop(1, count)
            def _(step):
                make(step).wait_recv()

        def send_all(make, count):
            @pl.loop(1, count)
            def _(step):
                make(step).wait_send()

        start_all(fa_copy, slabs)

        def attend(head):
            part = lanes(head)
            near_copy(head).wait_recv()
            far_copy(head).wait_recv()
            query, cot = aq[:, part], ao[:, part]
            key_all = kv[head, :, 0].reshape(keys, HEAD_DIM)
            value_all = kv[head, :, 1].reshape(keys, HEAD_DIM)
            scores = contract(key_all, query, 1, 1) * scale + bias[...]
            peak = jnp.max(scores, axis=0, keepdims=True)
            powers = jnp.exp(scores - peak)
            probs = powers * (1.0 / jnp.sum(powers, axis=0, keepdims=True))
            low = probs.astype(BF16)
            slope = contract(value_all, cot, 1, 1)
            offset = jnp.sum(low.astype(F32) * slope, axis=0, keepdims=True)
            score_grad = (probs * (slope - offset)).astype(BF16)
            daq[:, part] = (contract(score_grad, key_all, 0, 0) * scale).astype(BF16)
            grads[head, 0] = contract(score_grad, query, 1, 0) * scale
            grads[head, 1] = contract(low, cot, 1, 0)
            for place in range(2):
                rows = slice((2 * place + 1) * ROWS, (2 * place + 2) * ROWS)
                gs_out[head, place] = grads[head, :, rows].astype(BF16)
            gs_copy(head).start()

        def gs_copy(head):
            return copy(
                gs_out.at[head], gs_in.at[head], g_send.at[head, 0], g_recv.at[head, 0],
                {"ctx": sibling},
            )

        def g2_copy(head):
            return copy(
                g2_out.at[head], g2_in.at[head], g_send.at[head, 1], g_recv.at[head, 1],
                {"ctx": behind},
            )

        def g1_copy(head):
            return copy(
                g1_out.at[head], g1_in.at[head], g_send.at[head, 2], g_recv.at[head, 2],
                {"ctx": behind},
            )

        first_core = core == 0

        def return_two(head):
            gs_copy(head).wait_recv()
            mine = grads[head, :, 4 * ROWS : 5 * ROWS]
            theirs = gs_in[head, 1].astype(F32)
            g2_out[head] = (mine + jnp.where(first_core, 0.0, theirs)).astype(BF16)
            g2_copy(head).start()

        def return_one(head):
            g2_copy(head).wait_recv()
            mine = grads[head, :, 2 * ROWS : 3 * ROWS]
            theirs = jnp.where(first_core, gs_in[head, 1].astype(F32), gs_in[head, 0].astype(F32))
            g1_out[head] = (mine + theirs + g2_in[head].astype(F32)).astype(BF16)
            g1_copy(head).start()

        def return_own(head):
            part = lanes(head)
            g1_copy(head).wait_recv()
            mine = grads[head, :, 0:ROWS]
            theirs = jnp.where(first_core, gs_in[head, 0].astype(F32), 0.0)
            done = mine + theirs + g1_in[head].astype(F32)
            dak[:, part] = done[0].astype(BF16)
            dav[:, part] = done[1].astype(BF16)

        half = heads // 2

        @pl.loop(0, half)
        def _(head):
            attend(head)

        recv_all(fa_copy, slabs)
        slab_sum = ft[pl.ds(pl.multiple_of(slab * slab_taps, slab_taps), slab_taps), :]
        for step in range(1, slabs):
            slab_sum = slab_sum + fa_in[step - 1].astype(F32)
        for place in range(line):
            fb_out[place] = slab_sum[place * row_taps : (place + 1) * row_taps]
        start_all(fb_copy, line)

        @pl.loop(half, heads)
        def _(head):
            attend(head)
            return_two(head - half)

        recv_all(fb_copy, line)
        row_sum = fb_out[z]
        for step in range(1, line):
            row_sum = row_sum + fb_in[step - 1]
        fc[z] = row_sum * (n * ROWS) ** (-0.5)
        start_all(fc_copy, line)

        @pl.loop(half, heads)
        def _(head):
            return_two(head)

        sig_copy.wait_recv()
        sig[ROWS:, :] = sig_in[...].astype(F32)
        reach = 2 * ROWS - GROUP

        def spread(column):
            part = lanes(column)
            own = segcols[ROWS : 2 * ROWS, :]
            for r in range(GROUP):
                same = segcols[ROWS + r : ROWS + r + reach, :] == segcols[ROWS : ROWS + reach, :]
                back[r] = jnp.where(same, sig[r : r + reach, part], 0.0)

            def step(a, total):
                base = pl.multiple_of(GROUP * a, GROUP)
                coeff = taps_t[pl.ds(base, GROUP), part]
                term = coeff[0:1] * back[0, pl.ds(base, ROWS), :]
                for r in range(1, GROUP):
                    term = term + coeff[r : r + 1] * back[r, pl.ds(base, ROWS), :]
                same = segcols[pl.ds(pl.multiple_of(ROWS + base, GROUP), ROWS), :] == own
                return total + jnp.where(same, term, 0.0)

            found = lax.fori_loop(0, TAPS // GROUP, step, jnp.zeros((ROWS, LANES), F32))
            dhk[:, part] = (found * hv[:, part].astype(F32)).astype(BF16)
            dhv[:, part] = (found * hk[:, part].astype(F32)).astype(BF16)

        @pl.loop(0, columns)
        def _(column):
            spread(column)
            return_one(column)

        recv_all(fc_copy, line)
        fd[slab] = jnp.concatenate([fc[place] for place in range(line)]).astype(BF16)
        start_all(fd_copy, slabs)

        @pl.loop(0, heads)
        def _(head):
            return_own(head)

        recv_all(fd_copy, slabs)
        dfilter[...] = fd[...].reshape(TAPS, width).astype(F32).T

        halo_copy.wait_send()
        sig_copy.wait_send()
        for step in range(1, m):
            sum_copy(step).wait_send()

        @pl.loop(0, heads)
        def _(head):
            for made in (own_copy, pass_copy, near_copy, far_copy, gs_copy, g2_copy, g1_copy):
                made(head).wait_send()

        send_all(fa_copy, slabs)
        send_all(fb_copy, line)
        send_all(fc_copy, line)
        send_all(fd_copy, slabs)

    vmem = pltpu.VMEM
    dma = pltpu.SemaphoreType.DMA
    square = (ROWS, LANES)
    scratch = [
        vmem((ROWS, LANES), F32),
        vmem((3 * ROWS, LANES), F32),
        vmem((keys, ROWS), F32),
        vmem((TAPS, width), F32),
        vmem((2 * ROWS, width), F32),
        vmem((ROWS, width), BF16),
        vmem((ROWS, width), BF16),
        vmem((GROUP, 2 * ROWS, width), F32),
        vmem((ROWS, width), F32),
        vmem((ROWS, width), F32),
        vmem((ROWS, width), F32),
        vmem(square, F32),
        vmem(square, F32),
        vmem((8, ROWS), F32),
        vmem((max(1, m - 1), 8, ROWS), F32),
        vmem((2 * ROWS, width), F32),
        vmem((ROWS, width), BF16),
        vmem((ROWS, width), BF16),
        vmem((GROUP, 2 * ROWS - GROUP, LANES), F32),
        vmem((TAPS, width), F32),
        vmem((slabs, slab_taps, width), BF16),
        vmem((slabs - 1, slab_taps, width), BF16),
        vmem((line, row_taps, width), F32),
        vmem((line - 1, row_taps, width), F32),
        vmem((line, row_taps, width), F32),
        vmem((slabs, slab_taps, width), BF16),
        vmem((heads, SPAN + 1, 2, ROWS, HEAD_DIM), BF16),
        vmem((heads, 2, keys, HEAD_DIM), F32),
        vmem((heads, 2, 2, ROWS, HEAD_DIM), BF16),
        vmem((heads, 2, 2, ROWS, HEAD_DIM), BF16),
        vmem((heads, 2, ROWS, HEAD_DIM), BF16),
        vmem((heads, 2, ROWS, HEAD_DIM), BF16),
        vmem((heads, 2, ROWS, HEAD_DIM), BF16),
        vmem((heads, 2, ROWS, HEAD_DIM), BF16),
        dma((2,)),
        dma((2,)),
        dma((max(1, m - 1),)),
        dma((max(1, m - 1),)),
        dma((heads, 4)),
        dma((heads, 4)),
        dma((heads, 3)),
        dma((heads, 3)),
        dma((2, slabs - 1)),
        dma((2, slabs - 1)),
        dma((2, line - 1)),
        dma((2, line - 1)),
    ]
    return kernel, scratch


def build(mesh, line):
    n, m = mesh.shape["ctx"], mesh.shape["mp"]

    def body(aq, ak, av, ao, hq, hk, hv, ho, taps, gain, seg):
        rows, width = aq.shape
        kernel, scratch = make_kernel(n, m, width, line)
        wide = jax.ShapeDtypeStruct((rows, width), BF16)
        whole = pl.BlockSpec(memory_space=pltpu.VMEM)
        return pl.pallas_call(
            kernel,
            out_shape=(wide,) * 6 + (jax.ShapeDtypeStruct((width, TAPS), F32),),
            in_specs=[whole] * 11,
            out_specs=(whole,) * 7,
            scratch_shapes=scratch,
            compiler_params=pltpu.CompilerParams(
                collective_id=0, has_side_effects=True, vmem_limit_bytes=40 * 2**20
            ),
        )(aq, ak, av, ao, hq, hk, hv, ho, taps, gain.reshape(1, width), seg.reshape(n, rows))

    wide = P("ctx", "mp")
    return jax.shard_map(
        body,
        mesh=mesh,
        in_specs=(wide,) * 8 + (P("mp", None), P("mp"), P()),
        out_specs=(wide,) * 6 + (P("mp", None),),
        check_vma=False,
    )


def solution(mesh):
    return build(mesh, LINE)
```

```python
import jax
import jax.numpy as jnp
from jax import lax
from jax.experimental import pallas as pl
from jax.experimental.pallas import tpu as pltpu
from jax.sharding import PartitionSpec as P

SPAN = 4
HEAD_DIM = 128
TAPS = 128
ROWS = 128
LINE = 16
GROUP = 8
QUAD = 4
PART = 64
LANES = 128
F32 = jnp.float32
BF16 = jnp.bfloat16
FAR = -1e30
MESH = pl.DeviceIdType.MESH


def contract(left, right, left_dim, right_dim):
    return lax.dot_general(
        left, right, (((left_dim,), (right_dim,)), ((), ())), preferred_element_type=F32
    )


def fold(tiles, row):
    for bit in (4, 2, 1):
        low = (row & bit) == 0
        half = len(tiles) // 2
        folded = []
        for first, second in zip(tiles[:half], tiles[half:]):
            keep = jnp.where(low, first, second)
            move = jnp.where(low, second, first)
            up = pltpu.roll(move, 8 - bit, 0)
            folded.append(keep + (up if bit == 4 else jnp.where(low, up, pltpu.roll(move, bit, 0))))
        tiles = folded
    return tiles[0]


def make_kernel(n, m, width, line):
    heads = width // HEAD_DIM
    columns = width // LANES
    channels = width * m
    pairs = line // 2
    crew = 2 * n // line
    crew_taps = TAPS // crew
    chunks = columns // 2
    keys = (SPAN + 1) * ROWS
    scale = HEAD_DIM ** (-0.5)
    pieces = ROWS // PART
    quads = TAPS // GROUP // QUAD
    inner = [piece * PART // (GROUP * QUAD) if piece else 0 for piece in range(pieces)]

    def lanes(index):
        return pl.ds(pl.multiple_of(index * LANES, LANES), LANES)

    def kernel(
        aq_in, ak_in, av_in, ao_in, hq_in, hk_in, hv_in, ho_in, taps_in, gain_in, seg_in,
        daq_out, dak_out, dav_out, dhq_out, dhk_out, dhv_out, dfilter_out,
        daq, dak, dav, dhq, dhk, dhv, dfilter,
        aq, ao, hq, hk, hv, ho, taps, gain, seg,
        segrows, segcols, bias, taps_t, ext, halo_out, halo_in, shifts,
        mixed, gated, weighted, squares, crossed, sums, sums_in,
        sig, sig_out, sig_in, back, ft, fa_out, fa_in, fb, fd,
        kv, grads, gs_out, gs_in, g2_out, g2_in, g1_out, g1_in,
        load_sem, one_send, one_recv, mp_send, mp_recv, kv_send, kv_recv,
        g_send, g_recv, f_send, f_recv, token, store_sem,
    ):
        i = lax.axis_index("ctx")
        j = lax.axis_index("mp")
        core = lax.rem(i, 2)
        chip = i // 2
        z = lax.rem(chip, line)
        x = chip // line
        pair = z // 2
        member = (x * 2 + core) * 2 + lax.rem(z, 2)
        after, before = lax.rem(i + 1, n), lax.rem(i + n - 1, n)
        ahead, behind = lax.rem(i + 2, n), lax.rem(i + n - 2, n)
        far_ahead, far_behind = lax.rem(i + 4, n), lax.rem(i + n - 4, n)
        sibling = i + 1 - 2 * core

        def copy(src, dst, send, recv, device):
            return pltpu.make_async_remote_copy(
                src_ref=src, dst_ref=dst, send_sem=send, recv_sem=recv,
                device_id=device, device_id_type=MESH,
            )

        def at_line(steps):
            return {"ctx": (x * line + lax.rem(z + line + steps, line)) * 2 + core}

        def crew_peer(step):
            other = lax.rem(member + step, crew)
            spot = (other // 4) * line + pair * 2 + lax.rem(other, 2)
            return other, {"ctx": spot * 2 + lax.rem(other // 2, 2)}

        arrays = (
            (hk_in, hk), (hv_in, hv), (taps_in, taps), (seg_in, seg), (hq_in, hq), (ho_in, ho),
            (gain_in, gain), (aq_in, aq), (ao_in, ao),
        )
        loads = [
            pltpu.make_async_copy(src, dst, load_sem.at[place])
            for place, (src, dst) in enumerate(arrays)
        ]
        for head in range(heads):
            part = slice(head * HEAD_DIM, (head + 1) * HEAD_DIM)
            for place, src in enumerate((ak_in, av_in)):
                loads.append(
                    pltpu.make_async_copy(
                        src.at[:, part], kv.at[head, 0, place], load_sem.at[len(loads)]
                    )
                )
        hk_load, hv_load, taps_load, seg_load, hq_load, ho_load, gain_load, aq_load, ao_load = loads[:9]
        kv_loads = loads[9:]
        for load in (hk_load, hv_load, *kv_loads, seg_load, taps_load):
            load.start()
        for load in (hq_load, ho_load, gain_load, aq_load, ao_load):
            load.start()

        barrier = pltpu.get_barrier_semaphore()

        def greet(device):
            pl.semaphore_signal(barrier, inc=1, device_id=device, device_id_type=MESH)

        for device in (after, before, ahead, behind, far_ahead, far_behind, sibling):
            greet({"ctx": device})
        for step in range(1, m):
            greet({"mp": lax.rem(j + step, m)})
        greet(at_line(2))
        greet(at_line(-2))

        @pl.loop(1, crew)
        def _(step):
            greet(crew_peer(step)[1])

        stores = [
            pltpu.make_async_copy(src, dst, store_sem.at[place])
            for place, (src, dst) in enumerate((
                (daq, daq_out), (dak, dak_out), (dav, dav_out), (dhq, dhq_out), (dhk, dhk_out),
                (dhv, dhv_out), (dfilter, dfilter_out),
            ))
        ]

        hk_load.wait()
        hv_load.wait()
        product = hk[...].astype(F32) * hv[...].astype(F32)
        ext[ROWS:, :] = product
        halo_out[...] = product.astype(BF16)

        pl.semaphore_wait(barrier, 7 + (m - 1) + 2 + (crew - 1))

        halo_copy = copy(halo_out, halo_in, one_send.at[0], one_recv.at[0], {"ctx": after})
        halo_copy.start()

        def own_copy(head):
            return copy(
                kv.at[head, 0], kv.at[head, 2], kv_send.at[head, 0], kv_recv.at[head, 0],
                {"ctx": ahead},
            )

        def pass_copy(head):
            return copy(
                kv.at[head, 2], kv.at[head, 4], kv_send.at[head, 1], kv_recv.at[head, 1],
                {"ctx": ahead},
            )

        def near_copy(head):
            return copy(
                kv.at[head, 2 * core], kv.at[head, 1], kv_send.at[head, 2], kv_recv.at[head, 2],
                {"ctx": sibling},
            )

        def far_copy(head):
            return copy(
                kv.at[head, 2 * core + 2], kv.at[head, 3], kv_send.at[head, 3],
                kv_recv.at[head, 3], {"ctx": sibling},
            )

        def leap_copy(head):
            return copy(
                kv.at[head, 0], kv.at[head, 4], kv_send.at[head, 1], kv_recv.at[head, 1],
                {"ctx": far_ahead},
            )

        def tell(place, steps):
            for way in (steps, -steps):
                pl.semaphore_signal(
                    token.at[place], inc=1, device_id=at_line(way), device_id_type=MESH
                )

        tell(0, 2)

        def first_service(head):
            own_copy(head).wait_recv()
            if head:
                pass_copy(head).start()
            near_copy(head).start()

        def second_service(head):
            pass_copy(head).wait_recv()
            far_copy(head).start()

        seg_load.wait()
        segrows[...] = jnp.zeros_like(segrows)
        for row in range(SPAN + 2):
            block = i - SPAN + row
            inside = (block >= 0) & (block < n)
            held = seg[pl.ds(jnp.clip(block, 0, n - 1), 1), :]
            segrows[row : row + 1, :] = jnp.where(inside, held, -1 if row < SPAN else -2).astype(F32)
        turned = segrows[...].T
        for place in range(3):
            row = SPAN - 1 + place
            segcols[place * ROWS : (place + 1) * ROWS, :] = jnp.broadcast_to(
                turned[:, row : row + 1], (ROWS, LANES)
            )

        query_seg = segrows[SPAN : SPAN + 1, :]
        key_at = lax.broadcasted_iota(jnp.int32, (ROWS, ROWS), 0)
        query_at = lax.broadcasted_iota(jnp.int32, (ROWS, ROWS), 1)
        for back_by in range(SPAN + 1):
            row = SPAN - back_by
            allowed = turned[:, row : row + 1] == query_seg
            if back_by == 0:
                allowed = allowed & (key_at <= query_at)
            bias[back_by * ROWS : (back_by + 1) * ROWS, :] = jnp.where(allowed, 0.0, FAR)

        def shift_rows(start, stop):
            @pl.loop(0, columns)
            def _(column):
                part = lanes(column)
                for r in range(GROUP):
                    same = segcols[start - r : stop - r, :] == segcols[start:stop, :]
                    shifts[r, start:stop, part] = jnp.where(
                        same, ext[start - r : stop - r, part], 0.0
                    )

        shift_rows(ROWS + GROUP, 2 * ROWS)
        taps_load.wait()
        taps_t[...] = taps[...].T
        squares[...] = jnp.zeros_like(squares)
        crossed[...] = jnp.zeros_like(crossed)
        def tap_groups(column, piece, start, stop, total):
            part = lanes(column)
            own = segcols[ROWS + piece * PART : ROWS + (piece + 1) * PART, :]
            span = PART + GROUP * (QUAD - 1)

            def step(quad, total):
                first = pl.multiple_of(
                    ROWS + piece * PART - GROUP * (QUAD * quad + QUAD - 1), GROUP
                )
                begin = pl.multiple_of(GROUP * QUAD * quad, GROUP * QUAD)
                coeff = taps_t[pl.ds(begin, GROUP * QUAD), part]
                segs = segcols[pl.ds(first, span), :]
                terms = [None] * QUAD
                for r in range(GROUP):
                    block = shifts[r, pl.ds(first, span), part]
                    for k in range(QUAD):
                        off = GROUP * (QUAD - 1 - k)
                        at = GROUP * k + r
                        term = coeff[at : at + 1] * block[off : off + PART]
                        terms[k] = term if r == 0 else terms[k] + term
                for k in range(QUAD):
                    off = GROUP * (QUAD - 1 - k)
                    total = total + jnp.where(segs[off : off + PART] == own, terms[k], 0.0)
                return total

            return lax.fori_loop(start, stop, step, total)

        def convolve(column):
            part = lanes(column)
            for piece in range(pieces):
                rows = slice(piece * PART, (piece + 1) * PART)
                if piece == 0:
                    begun = jnp.zeros((PART, LANES), F32)
                else:
                    begun = mixed[rows, part]
                found = tap_groups(column, piece, inner[piece], quads, begun)
                mixed[rows, part] = found
                gate = hq[rows, part].astype(F32) * found
                heavy = gain[:, part] * ho[rows, part].astype(F32)
                gated[rows, part] = gate
                weighted[rows, part] = heavy
                squares[rows, :] += gate * gate
                crossed[rows, :] += heavy * gate

        def attend(head):
            part = lanes(head)
            near_copy(head).wait_recv()
            far_copy(head).wait_recv()
            query, cot = aq[:, part], ao[:, part]
            key_all = kv[head, :, 0].reshape(keys, HEAD_DIM)
            value_all = kv[head, :, 1].reshape(keys, HEAD_DIM)
            scores = contract(key_all, query, 1, 1) * scale + bias[...]
            peak = jnp.max(scores, axis=0, keepdims=True)
            powers = jnp.exp(scores - peak)
            probs = powers * (1.0 / jnp.sum(powers, axis=0, keepdims=True))
            low = probs.astype(BF16)
            slope = contract(value_all, cot, 1, 1)
            offset = jnp.sum(low.astype(F32) * slope, axis=0, keepdims=True)
            score_grad = (probs * (slope - offset)).astype(BF16)
            daq[:, part] = (contract(score_grad, key_all, 0, 0) * scale).astype(BF16)
            grads[head, 0] = contract(score_grad, query, 1, 0) * scale
            grads[head, 1] = contract(low, cot, 1, 0)
            for place in range(2):
                rows = slice((2 * place + 1) * ROWS, (2 * place + 2) * ROWS)
                gs_out[head, place] = grads[head, :, rows].astype(BF16)
            gs_copy(head).start()

        def gs_copy(head):
            return copy(
                gs_out.at[head], gs_in.at[head], g_send.at[head, 0], g_recv.at[head, 0],
                {"ctx": sibling},
            )

        def g2_copy(head):
            return copy(
                g2_out.at[head], g2_in.at[head], g_send.at[head, 1], g_recv.at[head, 1],
                {"ctx": behind},
            )

        def g1_copy(head):
            return copy(
                g1_out.at[head], g1_in.at[head], g_send.at[head, 2], g_recv.at[head, 2],
                {"ctx": behind},
            )

        first_core = core == 0

        def return_two(head):
            gs_copy(head).wait_recv()
            mine = grads[head, :, 4 * ROWS : 5 * ROWS]
            theirs = gs_in[head, 1].astype(F32)
            g2_out[head] = (mine + jnp.where(first_core, 0.0, theirs)).astype(BF16)
            g2_copy(head).start()

        def return_one(head):
            g2_copy(head).wait_recv()
            mine = grads[head, :, 2 * ROWS : 3 * ROWS]
            theirs = jnp.where(first_core, gs_in[head, 1].astype(F32), gs_in[head, 0].astype(F32))
            g1_out[head] = (mine + theirs + g2_in[head].astype(F32)).astype(BF16)
            g1_copy(head).start()

        def return_own(head):
            part = lanes(head)
            g1_copy(head).wait_recv()
            mine = grads[head, :, 0:ROWS]
            theirs = jnp.where(first_core, gs_in[head, 0].astype(F32), 0.0)
            done = mine + theirs + g1_in[head].astype(F32)
            dak[:, part] = done[0].astype(BF16)
            dav[:, part] = done[1].astype(BF16)

        @pl.loop(0, columns)
        def _(column):
            for piece in range(1, pieces):
                rows = slice(piece * PART, (piece + 1) * PART)
                mixed[rows, lanes(column)] = tap_groups(
                    column, piece, 0, inner[piece], jnp.zeros((PART, LANES), F32)
                )

        for load in (*kv_loads, hq_load, ho_load, gain_load):
            load.wait()
        own_copy(0).start()
        leap_copy(0).start()
        own_copy(1).start()

        halo_copy.wait_recv()
        ext[:ROWS, :] = halo_in[...].astype(F32)
        shift_rows(GROUP, ROWS + GROUP)

        @pl.loop(0, 2)
        def _(column):
            convolve(column)

        own_copy(2).start()

        @pl.loop(2, columns)
        def _(column):
            convolve(column)

        square_sum = jnp.sum(squares[...], axis=1, keepdims=True)
        cross_sum = jnp.sum(crossed[...], axis=1, keepdims=True)
        lane_at = lax.broadcasted_iota(jnp.int32, (ROWS, LANES), 1)
        squares[...] = jnp.where(lane_at == 0, square_sum, jnp.where(lane_at == 1, cross_sum, 0.0))
        sums[...] = squares[...].T[0:8]

        def sum_copy(step):
            return copy(
                sums, sums_in.at[step - 1], mp_send.at[step - 1], mp_recv.at[step - 1],
                {"mp": lax.rem(j + step, m)},
            )

        for step in range(1, m):
            sum_copy(step).start()

        pl.semaphore_wait(token.at[0], 2)
        tell(1, 4)
        own_copy(3).start()
        first_service(0)
        second_service(0)
        first_service(1)
        aq_load.wait()
        ao_load.wait()
        attend(0)
        for step in range(1, m):
            sum_copy(step).wait_recv()
        whole = sums[...]
        for step in range(1, m):
            whole = whole + sums_in[step - 1]
        inverse = lax.rsqrt(whole[0:1] / channels + 1e-06)
        factor = inverse * inverse * inverse * (whole[1:2] / channels)
        squares[0:1, :] = inverse
        squares[1:2, :] = factor
        upright = squares[...].T
        squares[...] = jnp.broadcast_to(upright[:, 0:1], (ROWS, LANES))
        crossed[...] = jnp.broadcast_to(upright[:, 1:2], (ROWS, LANES))

        @pl.loop(0, columns)
        def _(column):
            part = lanes(column)
            slope = squares[...] * weighted[:, part] - gated[:, part] * crossed[...]
            dhq[:, part] = (slope * mixed[:, part]).astype(BF16)
            signal = slope * hq[:, part].astype(F32)
            sig[:ROWS, part] = signal
            sig_out[:, part] = signal.astype(BF16)

        sig_copy = copy(sig_out, sig_in, one_send.at[1], one_recv.at[1], {"ctx": before})
        sig_copy.start()
        stores[3].start()

        def correlate(column):
            part = lanes(column)
            own = segcols[ROWS : 2 * ROWS, :]
            signal = sig[:ROWS, part]
            row = lax.broadcasted_iota(jnp.int32, (GROUP, LANES), 0)

            @pl.loop(0, quads)
            def _(quad):
                span = PART + GROUP * (QUAD - 1)
                for piece in range(pieces):
                    rows = slice(piece * PART, (piece + 1) * PART)
                    first = pl.multiple_of(
                        ROWS + piece * PART - GROUP * (QUAD * quad + QUAD - 1), GROUP
                    )
                    segs = segcols[pl.ds(first, span), :]
                    masked = [
                        jnp.where(segs[off : off + PART] == own[rows], signal[rows], 0.0)
                        for off in range(GROUP * (QUAD - 1), -1, -GROUP)
                    ]
                    found = [[] for _ in range(QUAD)]
                    for r in range(GROUP):
                        block = shifts[r, pl.ds(first, span), part]
                        for k in range(QUAD):
                            off = GROUP * (QUAD - 1 - k)
                            term = masked[k] * block[off : off + PART]
                            found[k].append(term.reshape(PART // 8, 8, LANES).sum(axis=0))
                    for k in range(QUAD):
                        begin = pl.multiple_of(GROUP * (QUAD * quad + k), GROUP)
                        total = fold(found[k], row)
                        if piece:
                            total = total + ft[pl.ds(begin, GROUP), part]
                        ft[pl.ds(begin, GROUP), part] = total

        def fa_copy(chunk, step):
            other, device = crew_peer(step)
            return copy(
                fa_out.at[chunk, other], fa_in.at[chunk, step - 1], f_send.at[0, chunk],
                f_recv.at[0, chunk], device,
            )

        def fb_copy(chunk, step):
            return copy(
                fb.at[chunk, pair], fb.at[chunk, pair], f_send.at[1, chunk],
                f_recv.at[1, chunk], at_line(2 * step),
            )

        def fd_copy(chunk, step):
            _, device = crew_peer(step)
            return copy(
                fd.at[chunk, member], fd.at[chunk, member], f_send.at[2, chunk],
                f_recv.at[2, chunk], device,
            )

        def wait_bytes(held, sems, phase, chunk, count):
            ref = held.at[chunk, pl.ds(0, count)]
            pltpu.make_async_copy(ref, ref, sems.at[phase, chunk]).wait()

        def start_all(make, chunk, count):
            @pl.loop(1, count)
            def _(step):
                make(chunk, step).start()

        def filter_out(chunk):
            for owner in range(crew):
                rows = slice(owner * crew_taps, (owner + 1) * crew_taps)
                tile = [ft[rows, lanes(2 * chunk + side)] for side in range(2)]
                fa_out[chunk, owner] = jnp.concatenate(tile).astype(BF16)
            start_all(fa_copy, chunk, crew)

        def filter_sum(chunk):
            wait_bytes(fa_in, f_recv, 0, chunk, crew - 1)
            rows = pl.ds(pl.multiple_of(member * crew_taps, crew_taps), crew_taps)
            total = jnp.concatenate([ft[rows, lanes(2 * chunk + side)] for side in range(2)])
            for step in range(1, crew):
                total = total + fa_in[chunk, step - 1].astype(F32)
            fb[chunk, pair] = total.astype(BF16)
            start_all(fb_copy, chunk, pairs)

        def filter_whole(chunk):
            wait_bytes(fb, f_recv, 1, chunk, pairs - 1)
            total = fb[chunk, 0].astype(F32)
            for place in range(1, pairs):
                total = total + fb[chunk, place].astype(F32)
            fd[chunk, member] = (total * (n * ROWS) ** (-0.5)).astype(BF16)
            start_all(fd_copy, chunk, crew)

        def filter_done(chunk):
            wait_bytes(fd, f_recv, 2, chunk, crew - 1)
            for side in range(2):
                rows = slice(side * crew_taps, (side + 1) * crew_taps)
                taps_row = fd[chunk, :, rows].astype(F32).reshape(TAPS, LANES)
                begin = (2 * chunk + side) * LANES
                dfilter[begin : begin + LANES, :] = taps_row.T

        def spread(column):
            part = lanes(column)
            reach = 2 * ROWS - GROUP
            for r in range(GROUP):
                same = segcols[ROWS + r : ROWS + r + reach, :] == segcols[ROWS : ROWS + reach, :]
                back[r] = jnp.where(same, sig[r : r + reach, part], 0.0)
            for piece in range(ROWS // PART):
                rows = slice(piece * PART, (piece + 1) * PART)
                own = segcols[ROWS + piece * PART : ROWS + (piece + 1) * PART, :]
                span = PART + GROUP * (QUAD - 1)

                def step(quad, total):
                    begin = pl.multiple_of(GROUP * QUAD * quad, GROUP * QUAD)
                    first = pl.multiple_of(piece * PART + begin, GROUP)
                    coeff = taps_t[pl.ds(begin, GROUP * QUAD), part]
                    segs = segcols[pl.ds(pl.multiple_of(ROWS + first, GROUP), span), :]
                    terms = [None] * QUAD
                    for r in range(GROUP):
                        block = back[r, pl.ds(first, span), :]
                        for k in range(QUAD):
                            at = GROUP * k + r
                            term = coeff[at : at + 1] * block[GROUP * k : GROUP * k + PART]
                            terms[k] = term if r == 0 else terms[k] + term
                    for k in range(QUAD):
                        same = segs[GROUP * k : GROUP * k + PART] == own
                        total = total + jnp.where(same, terms[k], 0.0)
                    return total

                found = lax.fori_loop(
                    0, TAPS // GROUP // QUAD, step, jnp.zeros((PART, LANES), F32)
                )
                dhk[rows, part] = (found * hv[rows, part].astype(F32)).astype(BF16)
                dhv[rows, part] = (found * hk[rows, part].astype(F32)).astype(BF16)

        correlate(0)
        first_service(2)
        return_two(0)
        correlate(1)
        filter_out(0)
        first_service(3)
        second_service(1)
        correlate(2)
        correlate(3)
        filter_out(1)
        second_service(2)
        return_one(0)
        attend(1)
        second_service(3)
        pl.semaphore_wait(token.at[1], 2)
        filter_sum(0)
        attend(2)
        return_two(1)
        sig_copy.wait_recv()
        sig[ROWS:, :] = sig_in[...].astype(F32)
        spread(0)
        return_two(2)
        filter_sum(1)
        attend(3)
        stores[0].start()
        return_one(1)
        spread(1)
        return_two(3)
        return_one(2)
        spread(2)
        spread(3)
        stores[4].start()
        stores[5].start()
        return_one(3)
        filter_whole(0)
        return_own(0)
        return_own(1)
        filter_whole(1)
        return_own(2)
        return_own(3)
        stores[1].start()
        stores[2].start()
        filter_done(0)
        filter_done(1)
        stores[6].start()

        halo_copy.wait_send()
        sig_copy.wait_send()
        for step in range(1, m):
            sum_copy(step).wait_send()

        @pl.loop(0, heads)
        def _(head):
            for made in (own_copy, pass_copy, near_copy, far_copy, gs_copy, g2_copy, g1_copy):
                made(head).wait_send()

        for chunk in range(chunks):
            wait_bytes(fa_in, f_send, 0, chunk, crew - 1)
            wait_bytes(fb, f_send, 1, chunk, pairs - 1)
            wait_bytes(fd, f_send, 2, chunk, crew - 1)
        for store in stores:
            store.wait()

    vmem = pltpu.VMEM
    dma = pltpu.SemaphoreType.DMA
    square = (ROWS, LANES)
    wide = vmem((ROWS, width), BF16)
    scratch = [
        wide, wide, wide, wide, wide, wide,
        vmem((width, TAPS), F32),
        wide, wide, wide, wide, wide, wide,
        vmem((width, TAPS), F32),
        vmem((1, width), F32),
        vmem((n, ROWS), jnp.int32),
        vmem((ROWS, LANES), F32),
        vmem((3 * ROWS, LANES), F32),
        vmem((keys, ROWS), F32),
        vmem((TAPS, width), F32),
        vmem((2 * ROWS, width), F32),
        wide,
        wide,
        vmem((GROUP, 2 * ROWS, width), F32),
        vmem((ROWS, width), F32),
        vmem((ROWS, width), F32),
        vmem((ROWS, width), F32),
        vmem(square, F32),
        vmem(square, F32),
        vmem((8, ROWS), F32),
        vmem((max(1, m - 1), 8, ROWS), F32),
        vmem((2 * ROWS, width), F32),
        wide,
        wide,
        vmem((GROUP, 2 * ROWS - GROUP, LANES), F32),
        vmem((TAPS, width), F32),
        vmem((chunks, crew, 2 * crew_taps, LANES), BF16),
        vmem((chunks, crew - 1, 2 * crew_taps, LANES), BF16),
        vmem((chunks, pairs, 2 * crew_taps, LANES), BF16),
        vmem((chunks, crew, 2 * crew_taps, LANES), BF16),
        vmem((heads, SPAN + 1, 2, ROWS, HEAD_DIM), BF16),
        vmem((heads, 2, keys, HEAD_DIM), F32),
        vmem((heads, 2, 2, ROWS, HEAD_DIM), BF16),
        vmem((heads, 2, 2, ROWS, HEAD_DIM), BF16),
        vmem((heads, 2, ROWS, HEAD_DIM), BF16),
        vmem((heads, 2, ROWS, HEAD_DIM), BF16),
        vmem((heads, 2, ROWS, HEAD_DIM), BF16),
        vmem((heads, 2, ROWS, HEAD_DIM), BF16),
        dma((9 + 2 * heads,)),
        dma((2,)),
        dma((2,)),
        dma((max(1, m - 1),)),
        dma((max(1, m - 1),)),
        dma((heads, 4)),
        dma((heads, 4)),
        dma((heads, 3)),
        dma((heads, 3)),
        dma((3, chunks)),
        dma((3, chunks)),
        pltpu.SemaphoreType.REGULAR((2,)),
        dma((7,)),
    ]
    return kernel, scratch


def write_out(*refs):
    count = (len(refs) - 1) // 3
    sources, results, held, sems = refs[:count], refs[count : 2 * count], refs[2 * count : -1], refs[-1]
    loads = [
        pltpu.make_async_copy(src, mid, sems.at[0, place])
        for place, (src, mid) in enumerate(zip(sources, held))
    ]
    stores = [
        pltpu.make_async_copy(mid, dst, sems.at[1, place])
        for place, (mid, dst) in enumerate(zip(held, results))
    ]
    for load in loads:
        load.start()
    for load, store in zip(loads, stores):
        load.wait()
        store.start()
    for store in stores:
        store.wait()


def build(mesh, line):
    n, m = mesh.shape["ctx"], mesh.shape["mp"]

    def body(aq, ak, av, ao, hq, hk, hv, ho, taps, gain, seg):
        rows, width = aq.shape
        kernel, scratch = make_kernel(n, m, width, line)
        wide = jax.ShapeDtypeStruct((rows, width), BF16)
        shapes = (wide,) * 6 + (jax.ShapeDtypeStruct((width, TAPS), F32),)
        far = pl.BlockSpec(memory_space=pltpu.HBM)
        found = pl.pallas_call(
            kernel,
            out_shape=shapes,
            in_specs=[far] * 11,
            out_specs=(far,) * 7,
            scratch_shapes=scratch,
            compiler_params=pltpu.CompilerParams(
                collective_id=0, has_side_effects=True, vmem_limit_bytes=60 * 2**20
            ),
        )(aq, ak, av, ao, hq, hk, hv, ho, taps, gain.reshape(1, width), seg.reshape(n, rows))
        return pl.pallas_call(
            write_out,
            out_shape=shapes,
            in_specs=[far] * 7,
            out_specs=(far,) * 7,
            scratch_shapes=[pltpu.VMEM(one.shape, one.dtype) for one in shapes]
            + [pltpu.SemaphoreType.DMA((2, 7))],
            compiler_params=pltpu.CompilerParams(vmem_limit_bytes=60 * 2**20),
        )(*found)

    wide = P("ctx", "mp")
    return jax.shard_map(
        body,
        mesh=mesh,
        in_specs=(wide,) * 8 + (P("mp", None), P("mp"), P()),
        out_specs=(wide,) * 6 + (P("mp", None),),
        check_vma=False,
    )


def solution(mesh):
    return build(mesh, LINE)
```

```python
import jax
import jax.numpy as jnp
from jax import lax
from jax.experimental import pallas as pl
from jax.experimental.pallas import tpu as pltpu
from jax.sharding import PartitionSpec as P

SPAN = 4
HEAD_DIM = 128
TAPS = 128
ROWS = 128
LINE = 16
GROUP = 8
QUAD = 4
PART = 64
LANES = 128
F32 = jnp.float32
BF16 = jnp.bfloat16
FAR = -1e30
MESH = pl.DeviceIdType.MESH


def contract(left, right, left_dim, right_dim):
    return lax.dot_general(
        left, right, (((left_dim,), (right_dim,)), ((), ())), preferred_element_type=F32
    )


def fold(tiles, row):
    for bit in (4, 2, 1):
        low = (row & bit) == 0
        half = len(tiles) // 2
        folded = []
        for first, second in zip(tiles[:half], tiles[half:]):
            keep = jnp.where(low, first, second)
            move = jnp.where(low, second, first)
            up = pltpu.roll(move, 8 - bit, 0)
            folded.append(keep + (up if bit == 4 else jnp.where(low, up, pltpu.roll(move, bit, 0))))
        tiles = folded
    return tiles[0]


def make_kernel(n, m, width, line):
    heads = width // HEAD_DIM
    columns = width // LANES
    channels = width * m
    pairs = line // 2
    crew = 2 * n // line
    crew_taps = TAPS // crew
    chunks = 1
    sides = columns // chunks
    keys = (SPAN + 1) * ROWS
    scale = HEAD_DIM ** (-0.5)
    pieces = ROWS // PART
    quads = TAPS // GROUP // QUAD
    inner = [piece * PART // (GROUP * QUAD) if piece else 0 for piece in range(pieces)]

    def lanes(index):
        return pl.ds(pl.multiple_of(index * LANES, LANES), LANES)

    def kernel(
        aq_in, ak_in, av_in, ao_in, hq_in, hk_in, hv_in, ho_in, taps_in, gain_in, seg_in,
        daq_out, dak_out, dav_out, dhq_out, dhk_out, dhv_out, dfilter_out,
        daq, dak, dav, dhq, dhk, dhv, dfilter,
        hq, hk, hv, ho, taps, gain, seg,
        segrows, segcols, bias, taps_t, ext, halo_out, halo_in, shifts,
        mixed, gated, weighted, squares, crossed, sums, sums_in,
        sig, sig_out, sig_in, back, ft, fa_out, fa_in, fb, fd,
        kv, qc, qc_in, dq_out, dq_in, grads, gs_out, gs_in, up_out, up_in, down_out, down_in,
        load_sem, one_send, one_recv, mp_send, mp_recv, kv_send, kv_recv,
        g_send, g_recv, f_send, f_recv, token, store_sem,
    ):
        i = lax.axis_index("ctx")
        j = lax.axis_index("mp")
        core = lax.rem(i, 2)
        chip = i // 2
        z = lax.rem(chip, line)
        x = chip // line
        pair = z // 2
        member = (x * 2 + core) * 2 + lax.rem(z, 2)
        after, before = lax.rem(i + 1, n), lax.rem(i + n - 1, n)
        ahead, behind = lax.rem(i + 2, n), lax.rem(i + n - 2, n)
        sibling = i + 1 - 2 * core

        def copy(src, dst, send, recv, device):
            return pltpu.make_async_remote_copy(
                src_ref=src, dst_ref=dst, send_sem=send, recv_sem=recv,
                device_id=device, device_id_type=MESH,
            )

        def at_line(steps):
            return {"ctx": (x * line + lax.rem(z + line + steps, line)) * 2 + core}

        def crew_peer(step):
            other = lax.rem(member + step, crew)
            spot = (other // 4) * line + pair * 2 + lax.rem(other, 2)
            return other, {"ctx": spot * 2 + lax.rem(other // 2, 2)}

        arrays = (
            (hk_in, hk), (hv_in, hv), (taps_in, taps), (seg_in, seg), (hq_in, hq), (ho_in, ho),
            (gain_in, gain),
        )
        loads = [
            pltpu.make_async_copy(src, dst, load_sem.at[place])
            for place, (src, dst) in enumerate(arrays)
        ]
        for head in range(heads):
            part = slice(head * HEAD_DIM, (head + 1) * HEAD_DIM)
            for src, dst in (
                (ak_in, kv.at[head, 2, 0]), (av_in, kv.at[head, 2, 1]),
                (aq_in, qc.at[head, 0]), (ao_in, qc.at[head, 1]),
            ):
                loads.append(pltpu.make_async_copy(src.at[:, part], dst, load_sem.at[len(loads)]))
        hk_load, hv_load, taps_load, seg_load, hq_load, ho_load, gain_load = loads[:7]
        head_loads = [loads[7 + 4 * head : 11 + 4 * head] for head in range(heads)]
        hk_load.start()
        hv_load.start()

        def at_x(steps):
            wide = crew // 4
            return {"ctx": (lax.rem(x + wide + steps, wide) * line + z) * 2 + core}

        def at_mp(steps):
            return {"mp": lax.rem(j + m + steps, m)}

        beside = [{"ctx": sibling}, at_line(1), at_line(-1)]
        if crew > 4:
            beside += [at_x(1), at_x(-1)]
        across = [at_mp(1), at_mp(-1)] if m > 1 else []
        greeted = beside + across + [{"ctx": one} for one in (after, before, ahead, behind)]
        rounds = [
            beside + across,
            beside + [at_line(2), at_line(-2)],
            [{"ctx": sibling}, at_line(4), at_line(-4)],
        ]
        barrier = pltpu.get_barrier_semaphore()
        for device in greeted:
            pl.semaphore_signal(barrier, inc=1, device_id=device, device_id_type=MESH)

        def tell(place):
            for device in rounds[place]:
                pl.semaphore_signal(token.at[place], inc=1, device_id=device, device_id_type=MESH)

        def hear(place):
            pl.semaphore_wait(token.at[place], len(rounds[place]))

        for load in (*head_loads[0], *head_loads[1]):
            load.start()
        stores = [
            pltpu.make_async_copy(src, dst, store_sem.at[place])
            for place, (src, dst) in enumerate((
                (daq, daq_out), (dak, dak_out), (dav, dav_out), (dhq, dhq_out), (dhk, dhk_out),
                (dhv, dhv_out), (dfilter, dfilter_out),
            ))
        ]


        hk_load.wait()
        hv_load.wait()
        product = hk[...].astype(F32) * hv[...].astype(F32)
        ext[ROWS:, :] = product
        for half in range(2):
            part = slice(half * width // 2, (half + 1) * width // 2)
            halo_out[half] = product[:, part].astype(BF16)

        pl.semaphore_wait(barrier, len(greeted))

        def halo_copy(half):
            return copy(
                halo_out.at[half], halo_in.at[half], one_send.at[half], one_recv.at[half],
                {"ctx": after},
            )

        halo_copy(0).start()
        halo_copy(1).start()
        for load in (seg_load, taps_load, *loads[15:], hq_load, ho_load, gain_load):
            load.start()

        def give_back(head):
            return copy(
                kv.at[head, 2], kv.at[head, 0], kv_send.at[head, 0], kv_recv.at[head, 0],
                {"ctx": behind},
            )

        def give_queries(head):
            return copy(
                qc.at[head], qc_in.at[head], kv_send.at[head, 1], kv_recv.at[head, 1],
                {"ctx": behind},
            )

        def give_on(head):
            return copy(
                kv.at[head, 2], kv.at[head, 4], kv_send.at[head, 2], kv_recv.at[head, 2],
                {"ctx": ahead},
            )

        def near_copy(head):
            return copy(
                kv.at[head, 2 * core], kv.at[head, 1], kv_send.at[head, 3], kv_recv.at[head, 3],
                {"ctx": sibling},
            )

        def far_copy(head):
            return copy(
                kv.at[head, 2 * core + 2], kv.at[head, 3], kv_send.at[head, 4],
                kv_recv.at[head, 4], {"ctx": sibling},
            )

        def send_back(head):
            for load in head_loads[head]:
                load.wait()
            give_back(head).start()
            give_queries(head).start()

        send_back(0)

        tell(0)

        def service(head):
            give_back(head).wait_recv()
            give_on(head).wait_recv()
            near_copy(head).start()
            far_copy(head).start()

        seg_load.wait()
        segrows[...] = jnp.zeros_like(segrows)
        asked = lax.rem(i + 2, n)
        spots = [asked - back_by for back_by in range(SPAN, -1, -1)] + [i - 1, i, i + 1]
        for row, block in enumerate(spots):
            inside = (block >= 0) & (block < n)
            held = seg[pl.ds(jnp.clip(block, 0, n - 1), 1), :]
            outside = -2 if row == SPAN + 3 else -1
            segrows[row : row + 1, :] = jnp.where(inside, held, outside).astype(F32)
        turned = segrows[...].T
        for place in range(3):
            row = SPAN + 1 + place
            segcols[place * ROWS : (place + 1) * ROWS, :] = jnp.broadcast_to(
                turned[:, row : row + 1], (ROWS, LANES)
            )

        query_seg = segrows[SPAN : SPAN + 1, :]
        key_at = lax.broadcasted_iota(jnp.int32, (ROWS, ROWS), 0)
        query_at = lax.broadcasted_iota(jnp.int32, (ROWS, ROWS), 1)
        for back_by in range(SPAN + 1):
            row = SPAN - back_by
            allowed = turned[:, row : row + 1] == query_seg
            if back_by == 0:
                allowed = allowed & (key_at <= query_at)
            bias[back_by * ROWS : (back_by + 1) * ROWS, :] = jnp.where(allowed, 0.0, FAR)

        def shift_rows(start, stop, begin, end):
            @pl.loop(begin, end)
            def _(column):
                part = lanes(column)
                for r in range(GROUP):
                    same = segcols[start - r : stop - r, :] == segcols[start:stop, :]
                    shifts[r, start:stop, part] = jnp.where(
                        same, ext[start - r : stop - r, part], 0.0
                    )

        shift_rows(ROWS + GROUP, 2 * ROWS, 0, columns)
        taps_load.wait()
        taps_t[...] = taps[...].T
        squares[...] = jnp.zeros_like(squares)
        crossed[...] = jnp.zeros_like(crossed)
        def tap_groups(column, piece, start, stop, total):
            part = lanes(column)
            own = segcols[ROWS + piece * PART : ROWS + (piece + 1) * PART, :]
            span = PART + GROUP * (QUAD - 1)

            def step(quad, total):
                first = pl.multiple_of(
                    ROWS + piece * PART - GROUP * (QUAD * quad + QUAD - 1), GROUP
                )
                begin = pl.multiple_of(GROUP * QUAD * quad, GROUP * QUAD)
                coeff = taps_t[pl.ds(begin, GROUP * QUAD), part]
                segs = segcols[pl.ds(first, span), :]
                terms = [None] * QUAD
                for r in range(GROUP):
                    block = shifts[r, pl.ds(first, span), part]
                    for k in range(QUAD):
                        off = GROUP * (QUAD - 1 - k)
                        at = GROUP * k + r
                        term = coeff[at : at + 1] * block[off : off + PART]
                        terms[k] = term if r == 0 else terms[k] + term
                for k in range(QUAD):
                    off = GROUP * (QUAD - 1 - k)
                    total = total + jnp.where(segs[off : off + PART] == own, terms[k], 0.0)
                return total

            return lax.fori_loop(start, stop, step, total)

        def convolve(column):
            part = lanes(column)
            for piece in range(pieces):
                rows = slice(piece * PART, (piece + 1) * PART)
                if piece == 0:
                    begun = jnp.zeros((PART, LANES), F32)
                else:
                    begun = mixed[rows, part]
                found = tap_groups(column, piece, inner[piece], quads, begun)
                mixed[rows, part] = found
                gate = hq[rows, part].astype(F32) * found
                heavy = gain[:, part] * ho[rows, part].astype(F32)
                gated[rows, part] = gate
                weighted[rows, part] = heavy
                squares[rows, :] += gate * gate
                crossed[rows, :] += heavy * gate

        def attend(head):
            near_copy(head).wait_recv()
            far_copy(head).wait_recv()
            give_queries(head).wait_recv()
            query, cot = qc_in[head, 0], qc_in[head, 1]
            key_all = kv[head, :, 0].reshape(keys, HEAD_DIM)
            value_all = kv[head, :, 1].reshape(keys, HEAD_DIM)
            scores = contract(key_all, query, 1, 1) * scale + bias[...]
            peak = jnp.max(scores, axis=0, keepdims=True)
            powers = jnp.exp(scores - peak)
            probs = powers * (1.0 / jnp.sum(powers, axis=0, keepdims=True))
            low = probs.astype(BF16)
            slope = contract(value_all, cot, 1, 1)
            offset = jnp.sum(low.astype(F32) * slope, axis=0, keepdims=True)
            score_grad = (probs * (slope - offset)).astype(BF16)
            dq_out[head] = (contract(score_grad, key_all, 0, 0) * scale).astype(BF16)
            grads[head, 0] = contract(score_grad, query, 1, 0) * scale
            grads[head, 1] = contract(low, cot, 1, 0)
            for place in range(2):
                rows = slice((2 * place + 1) * ROWS, (2 * place + 2) * ROWS)
                gs_out[head, place] = grads[head, :, rows].astype(BF16)
            gs_copy(head).start()

        def gs_copy(head):
            return copy(
                gs_out.at[head], gs_in.at[head], g_send.at[head, 0], g_recv.at[head, 0],
                {"ctx": sibling},
            )

        def dq_copy(head):
            return copy(
                dq_out.at[head], dq_in.at[head], g_send.at[head, 1], g_recv.at[head, 1],
                {"ctx": ahead},
            )

        def up_copy(head):
            return copy(
                up_out.at[head], up_in.at[head], g_send.at[head, 2], g_recv.at[head, 2],
                {"ctx": ahead},
            )

        def down_copy(head):
            return copy(
                down_out.at[head], down_in.at[head], g_send.at[head, 3], g_recv.at[head, 3],
                {"ctx": behind},
            )

        first_core = core == 0

        def give_grads(head):
            gs_copy(head).wait_recv()
            near = gs_in[head, 0].astype(F32)
            far = gs_in[head, 1].astype(F32)
            ours = grads[head, :, 0:ROWS]
            up_out[head] = (ours + jnp.where(first_core, near, 0.0)).astype(BF16)
            up_copy(head).start()
            ours = grads[head, :, 4 * ROWS : 5 * ROWS]
            down_out[head] = (ours + jnp.where(first_core, 0.0, far)).astype(BF16)
            down_copy(head).start()
            dq_copy(head).start()

        def take_grads(head):
            part = slice(head * HEAD_DIM, (head + 1) * HEAD_DIM)
            ours = grads[head, :, 2 * ROWS : 3 * ROWS]
            theirs = jnp.where(first_core, gs_in[head, 1].astype(F32), gs_in[head, 0].astype(F32))
            down_copy(head).wait_recv()
            up_copy(head).wait_recv()
            dq_copy(head).wait_recv()
            done = ours + theirs + up_in[head].astype(F32) + down_in[head].astype(F32)
            daq[:, part] = dq_in[head]
            dak[:, part] = done[0].astype(BF16)
            dav[:, part] = done[1].astype(BF16)

        @pl.loop(0, columns)
        def _(column):
            for piece in range(1, pieces):
                rows = slice(piece * PART, (piece + 1) * PART)
                mixed[rows, lanes(column)] = tap_groups(
                    column, piece, 0, inner[piece], jnp.zeros((PART, LANES), F32)
                )

        for load in (hq_load, ho_load, gain_load):
            load.wait()
        give_on(0).start()
        send_back(1)
        hear(0)
        tell(1)

        for half in range(2):
            part = slice(half * width // 2, (half + 1) * width // 2)
            halo_copy(half).wait_recv()
            if half == 0:
                give_on(1).start()
            else:
                send_back(2)
                give_on(2).start()
            ext[:ROWS, part] = halo_in[half].astype(F32)
            begin, end = half * columns // 2, (half + 1) * columns // 2
            shift_rows(GROUP, ROWS + GROUP, begin, end)

            @pl.loop(begin, end)
            def _(column):
                convolve(column)

        square_sum = jnp.sum(squares[...], axis=1, keepdims=True)
        cross_sum = jnp.sum(crossed[...], axis=1, keepdims=True)
        lane_at = lax.broadcasted_iota(jnp.int32, (ROWS, LANES), 1)
        squares[...] = jnp.where(lane_at == 0, square_sum, jnp.where(lane_at == 1, cross_sum, 0.0))
        sums[...] = squares[...].T[0:8]

        def sum_copy(step):
            return copy(
                sums, sums_in.at[step - 1], mp_send.at[step - 1], mp_recv.at[step - 1],
                {"mp": lax.rem(j + step, m)},
            )

        for step in range(1, m):
            sum_copy(step).start()

        hear(1)
        tell(2)
        send_back(3)
        give_on(3).start()
        service(0)
        attend(0)
        for step in range(1, m):
            sum_copy(step).wait_recv()
        whole = sums[...]
        for step in range(1, m):
            whole = whole + sums_in[step - 1]
        inverse = lax.rsqrt(whole[0:1] / channels + 1e-06)
        factor = inverse * inverse * inverse * (whole[1:2] / channels)
        squares[0:1, :] = inverse
        squares[1:2, :] = factor
        upright = squares[...].T
        squares[...] = jnp.broadcast_to(upright[:, 0:1], (ROWS, LANES))
        crossed[...] = jnp.broadcast_to(upright[:, 1:2], (ROWS, LANES))

        @pl.loop(0, columns)
        def _(column):
            part = lanes(column)
            slope = squares[...] * weighted[:, part] - gated[:, part] * crossed[...]
            dhq[:, part] = (slope * mixed[:, part]).astype(BF16)
            signal = slope * hq[:, part].astype(F32)
            sig[:ROWS, part] = signal
            sig_out[:, part] = signal.astype(BF16)

        sig_copy = copy(sig_out, sig_in, one_send.at[2], one_recv.at[2], {"ctx": before})
        sig_copy.start()
        stores[3].start()
        def correlate(column):
            part = lanes(column)
            own = segcols[ROWS : 2 * ROWS, :]
            signal = sig[:ROWS, part]
            row = lax.broadcasted_iota(jnp.int32, (GROUP, LANES), 0)

            @pl.loop(0, quads)
            def _(quad):
                span = PART + GROUP * (QUAD - 1)
                for piece in range(pieces):
                    rows = slice(piece * PART, (piece + 1) * PART)
                    first = pl.multiple_of(
                        ROWS + piece * PART - GROUP * (QUAD * quad + QUAD - 1), GROUP
                    )
                    segs = segcols[pl.ds(first, span), :]
                    masked = [
                        jnp.where(segs[off : off + PART] == own[rows], signal[rows], 0.0)
                        for off in range(GROUP * (QUAD - 1), -1, -GROUP)
                    ]
                    found = [[] for _ in range(QUAD)]
                    for r in range(GROUP):
                        block = shifts[r, pl.ds(first, span), part]
                        for k in range(QUAD):
                            off = GROUP * (QUAD - 1 - k)
                            term = masked[k] * block[off : off + PART]
                            found[k].append(term.reshape(PART // 8, 8, LANES).sum(axis=0))
                    for k in range(QUAD):
                        begin = pl.multiple_of(GROUP * (QUAD * quad + k), GROUP)
                        total = fold(found[k], row)
                        if piece:
                            total = total + ft[pl.ds(begin, GROUP), part]
                        ft[pl.ds(begin, GROUP), part] = total

        def fa_copy(chunk, step):
            other, device = crew_peer(step)
            return copy(
                fa_out.at[chunk, other], fa_in.at[chunk, step - 1], f_send.at[0, chunk],
                f_recv.at[0, chunk], device,
            )

        def fb_copy(chunk, step):
            return copy(
                fb.at[chunk, pair], fb.at[chunk, pair], f_send.at[1, chunk],
                f_recv.at[1, chunk], at_line(2 * step),
            )

        def fd_copy(chunk, step):
            _, device = crew_peer(step)
            return copy(
                fd.at[chunk, member], fd.at[chunk, member], f_send.at[2, chunk],
                f_recv.at[2, chunk], device,
            )

        def wait_bytes(held, sems, phase, chunk, count):
            ref = held.at[chunk, pl.ds(0, count)]
            pltpu.make_async_copy(ref, ref, sems.at[phase, chunk]).wait()

        def start_all(make, chunk, count):
            @pl.loop(1, count)
            def _(step):
                make(chunk, step).start()

        def filter_out(chunk):
            for owner in range(crew):
                rows = slice(owner * crew_taps, (owner + 1) * crew_taps)
                tile = [ft[rows, lanes(sides * chunk + side)] for side in range(sides)]
                fa_out[chunk, owner] = jnp.concatenate(tile).astype(BF16)
            start_all(fa_copy, chunk, crew)

        def filter_sum(chunk):
            wait_bytes(fa_in, f_recv, 0, chunk, crew - 1)
            rows = pl.ds(pl.multiple_of(member * crew_taps, crew_taps), crew_taps)
            tile = [ft[rows, lanes(sides * chunk + side)] for side in range(sides)]
            total = jnp.concatenate(tile)
            for step in range(1, crew):
                total = total + fa_in[chunk, step - 1].astype(F32)
            fb[chunk, pair] = total.astype(BF16)
            for step in sorted(range(1, pairs), key=lambda step: -min(step, pairs - step)):
                fb_copy(chunk, step).start()

        def filter_whole(chunk):
            wait_bytes(fb, f_recv, 1, chunk, pairs - 1)
            total = fb[chunk, 0].astype(F32)
            for place in range(1, pairs):
                total = total + fb[chunk, place].astype(F32)
            fd[chunk, member] = (total * (n * ROWS) ** (-0.5)).astype(BF16)
            start_all(fd_copy, chunk, crew)

        def filter_done(chunk):
            wait_bytes(fd, f_recv, 2, chunk, crew - 1)
            for side in range(sides):
                rows = slice(side * crew_taps, (side + 1) * crew_taps)
                taps_row = fd[chunk, :, rows].astype(F32).reshape(TAPS, LANES)
                begin = (sides * chunk + side) * LANES
                dfilter[begin : begin + LANES, :] = taps_row.T

        def spread(column):
            part = lanes(column)
            reach = 2 * ROWS - GROUP
            for r in range(GROUP):
                same = segcols[ROWS + r : ROWS + r + reach, :] == segcols[ROWS : ROWS + reach, :]
                back[r] = jnp.where(same, sig[r : r + reach, part], 0.0)
            for piece in range(ROWS // PART):
                rows = slice(piece * PART, (piece + 1) * PART)
                own = segcols[ROWS + piece * PART : ROWS + (piece + 1) * PART, :]
                span = PART + GROUP * (QUAD - 1)

                def step(quad, total):
                    begin = pl.multiple_of(GROUP * QUAD * quad, GROUP * QUAD)
                    first = pl.multiple_of(piece * PART + begin, GROUP)
                    coeff = taps_t[pl.ds(begin, GROUP * QUAD), part]
                    segs = segcols[pl.ds(pl.multiple_of(ROWS + first, GROUP), span), :]
                    terms = [None] * QUAD
                    for r in range(GROUP):
                        block = back[r, pl.ds(first, span), :]
                        for k in range(QUAD):
                            at = GROUP * k + r
                            term = coeff[at : at + 1] * block[GROUP * k : GROUP * k + PART]
                            terms[k] = term if r == 0 else terms[k] + term
                    for k in range(QUAD):
                        same = segs[GROUP * k : GROUP * k + PART] == own
                        total = total + jnp.where(same, terms[k], 0.0)
                    return total

                found = lax.fori_loop(
                    0, TAPS // GROUP // QUAD, step, jnp.zeros((PART, LANES), F32)
                )
                dhk[rows, part] = (found * hv[rows, part].astype(F32)).astype(BF16)
                dhv[rows, part] = (found * hk[rows, part].astype(F32)).astype(BF16)

        correlate(0)
        give_grads(0)
        service(1)
        correlate(1)
        service(2)
        correlate(2)
        correlate(3)
        hear(2)
        filter_out(0)
        attend(1)
        service(3)
        attend(2)
        give_grads(1)
        attend(3)
        filter_sum(0)
        give_grads(2)
        sig_copy.wait_recv()
        sig[ROWS:, :] = sig_in[...].astype(F32)
        spread(0)
        give_grads(3)
        spread(1)
        spread(2)
        spread(3)
        stores[4].start()
        stores[5].start()
        take_grads(0)
        filter_whole(0)
        take_grads(1)
        take_grads(2)
        take_grads(3)
        for place in range(3):
            stores[place].start()

        halo_copy(0).wait_send()
        halo_copy(1).wait_send()
        sig_copy.wait_send()
        for step in range(1, m):
            sum_copy(step).wait_send()
        for head in range(heads):
            for made in (
                give_back, give_queries, give_on, near_copy, far_copy, gs_copy, dq_copy, up_copy,
                down_copy,
            ):
                made(head).wait_send()
        for chunk in range(chunks):
            wait_bytes(fa_in, f_send, 0, chunk, crew - 1)
            wait_bytes(fb, f_send, 1, chunk, pairs - 1)
        for chunk in range(chunks):
            filter_done(chunk)
            wait_bytes(fd, f_send, 2, chunk, crew - 1)
        stores[6].start()
        for store in stores:
            store.wait()

    vmem = pltpu.VMEM
    dma = pltpu.SemaphoreType.DMA
    square = (ROWS, LANES)
    wide = vmem((ROWS, width), BF16)
    scratch = [
        wide, wide, wide, wide, wide, wide,
        vmem((width, TAPS), F32),
        wide, wide, wide, wide,
        vmem((width, TAPS), F32),
        vmem((1, width), F32),
        vmem((n, ROWS), jnp.int32),
        vmem((ROWS, LANES), F32),
        vmem((3 * ROWS, LANES), F32),
        vmem((keys, ROWS), F32),
        vmem((TAPS, width), F32),
        vmem((2 * ROWS, width), F32),
        vmem((2, ROWS, width // 2), BF16),
        vmem((2, ROWS, width // 2), BF16),
        vmem((GROUP, 2 * ROWS, width), F32),
        vmem((ROWS, width), F32),
        vmem((ROWS, width), F32),
        vmem((ROWS, width), F32),
        vmem(square, F32),
        vmem(square, F32),
        vmem((8, ROWS), F32),
        vmem((max(1, m - 1), 8, ROWS), F32),
        vmem((2 * ROWS, width), F32),
        wide,
        wide,
        vmem((GROUP, 2 * ROWS - GROUP, LANES), F32),
        vmem((TAPS, width), F32),
        vmem((chunks, crew, sides * crew_taps, LANES), BF16),
        vmem((chunks, crew - 1, sides * crew_taps, LANES), BF16),
        vmem((chunks, pairs, sides * crew_taps, LANES), BF16),
        vmem((chunks, crew, sides * crew_taps, LANES), BF16),
        vmem((heads, SPAN + 1, 2, ROWS, HEAD_DIM), BF16),
        vmem((heads, 2, ROWS, HEAD_DIM), BF16),
        vmem((heads, 2, ROWS, HEAD_DIM), BF16),
        vmem((heads, ROWS, HEAD_DIM), BF16),
        vmem((heads, ROWS, HEAD_DIM), BF16),
        vmem((heads, 2, keys, HEAD_DIM), F32),
        vmem((heads, 2, 2, ROWS, HEAD_DIM), BF16),
        vmem((heads, 2, 2, ROWS, HEAD_DIM), BF16),
        vmem((heads, 2, ROWS, HEAD_DIM), BF16),
        vmem((heads, 2, ROWS, HEAD_DIM), BF16),
        vmem((heads, 2, ROWS, HEAD_DIM), BF16),
        vmem((heads, 2, ROWS, HEAD_DIM), BF16),
        dma((7 + 4 * heads,)),
        dma((3,)),
        dma((3,)),
        dma((max(1, m - 1),)),
        dma((max(1, m - 1),)),
        dma((heads, 5)),
        dma((heads, 5)),
        dma((heads, 4)),
        dma((heads, 4)),
        dma((3, chunks)),
        dma((3, chunks)),
        pltpu.SemaphoreType.REGULAR((3,)),
        dma((7,)),
    ]
    return kernel, scratch


def write_out(*refs):
    count = (len(refs) - 1) // 3
    sources, results, held, sems = refs[:count], refs[count : 2 * count], refs[2 * count : -1], refs[-1]
    loads = [
        pltpu.make_async_copy(src, mid, sems.at[0, place])
        for place, (src, mid) in enumerate(zip(sources, held))
    ]
    stores = [
        pltpu.make_async_copy(mid, dst, sems.at[1, place])
        for place, (mid, dst) in enumerate(zip(held, results))
    ]
    for load in loads:
        load.start()
    for load, store in zip(loads, stores):
        load.wait()
        store.start()
    for store in stores:
        store.wait()


def build(mesh, line):
    n, m = mesh.shape["ctx"], mesh.shape["mp"]

    def body(aq, ak, av, ao, hq, hk, hv, ho, taps, gain, seg):
        rows, width = aq.shape
        kernel, scratch = make_kernel(n, m, width, line)
        wide = jax.ShapeDtypeStruct((rows, width), BF16)
        shapes = (wide,) * 6 + (jax.ShapeDtypeStruct((width, TAPS), F32),)
        far = pl.BlockSpec(memory_space=pltpu.HBM)
        found = pl.pallas_call(
            kernel,
            out_shape=shapes,
            in_specs=[far] * 11,
            out_specs=(far,) * 7,
            scratch_shapes=scratch,
            compiler_params=pltpu.CompilerParams(
                collective_id=0, has_side_effects=True, vmem_limit_bytes=60 * 2**20
            ),
        )(aq, ak, av, ao, hq, hk, hv, ho, taps, gain.reshape(1, width), seg.reshape(n, rows))
        return pl.pallas_call(
            write_out,
            out_shape=shapes,
            in_specs=[far] * 7,
            out_specs=(far,) * 7,
            scratch_shapes=[pltpu.VMEM(one.shape, one.dtype) for one in shapes]
            + [pltpu.SemaphoreType.DMA((2, 7))],
            compiler_params=pltpu.CompilerParams(vmem_limit_bytes=60 * 2**20),
        )(*found)

    wide = P("ctx", "mp")
    return jax.shard_map(
        body,
        mesh=mesh,
        in_specs=(wide,) * 8 + (P("mp", None), P("mp"), P()),
        out_specs=(wide,) * 6 + (P("mp", None),),
        check_vma=False,
    )


def solution(mesh):
    return build(mesh, LINE)
```

```python
import jax
import jax.numpy as jnp
from jax import lax
from jax.experimental import pallas as pl
from jax.experimental.pallas import tpu as pltpu
from jax.sharding import PartitionSpec as P

SPAN = 4
HEAD_DIM = 128
TAPS = 128
ROWS = 128
LINE = 16
GROUP = 8
QUAD = 4
PART = 64
LANES = 128
F32 = jnp.float32
BF16 = jnp.bfloat16
FAR = -1e30
MESH = pl.DeviceIdType.MESH


def contract(left, right, left_dim, right_dim):
    return lax.dot_general(
        left, right, (((left_dim,), (right_dim,)), ((), ())), preferred_element_type=F32
    )


def fold(tiles, row):
    for bit in (4, 2, 1):
        low = (row & bit) == 0
        half = len(tiles) // 2
        folded = []
        for first, second in zip(tiles[:half], tiles[half:]):
            keep = jnp.where(low, first, second)
            move = jnp.where(low, second, first)
            up = pltpu.roll(move, 8 - bit, 0)
            folded.append(keep + (up if bit == 4 else jnp.where(low, up, pltpu.roll(move, bit, 0))))
        tiles = folded
    return tiles[0]


def make_kernel(n, m, width, line):
    heads = width // HEAD_DIM
    columns = width // LANES
    channels = width * m
    pairs = line // 2
    crew = 2 * n // line
    crew_taps = TAPS // crew
    chunks = 1
    sides = columns // chunks
    keys = (SPAN + 1) * ROWS
    scale = HEAD_DIM ** (-0.5)
    pieces = ROWS // PART
    quads = TAPS // GROUP // QUAD
    inner = [piece * PART // (GROUP * QUAD) if piece else 0 for piece in range(pieces)]

    def lanes(index):
        return pl.ds(pl.multiple_of(index * LANES, LANES), LANES)

    def kernel(
        aq_in, ak_in, av_in, ao_in, hq_in, hk_in, hv_in, ho_in, taps_in, gain_in, seg_in,
        daq_out, dak_out, dav_out, dhq_out, dhk_out, dhv_out, dfilter_out,
        daq, dak, dav, dhq, dhk, dhv,
        hq, hk, hv, ho, taps, gain, seg,
        segrows, segcols, bias, taps_t, ext, halo_out, halo_in, shifts,
        mixed, gated, weighted, squares, crossed, sums, sums_in,
        sig, sig_out, sig_in, back, ft, fa_out, fa_in, fb, fd,
        kv, qc, qc_in, dq_out, dq_in, grads, gs_out, gs_in, up_out, up_in, down_out, down_in,
        load_sem, one_send, one_recv, mp_send, mp_recv, kv_send, kv_recv,
        g_send, g_recv, f_send, f_recv, token, store_sem,
    ):
        i = lax.axis_index("ctx")
        j = lax.axis_index("mp")
        core = lax.rem(i, 2)
        chip = i // 2
        z = lax.rem(chip, line)
        x = chip // line
        pair = z // 2
        member = (x * 2 + core) * 2 + lax.rem(z, 2)
        after, before = lax.rem(i + 1, n), lax.rem(i + n - 1, n)
        ahead, behind = lax.rem(i + 2, n), lax.rem(i + n - 2, n)
        sibling = i + 1 - 2 * core

        def copy(src, dst, send, recv, device):
            return pltpu.make_async_remote_copy(
                src_ref=src, dst_ref=dst, send_sem=send, recv_sem=recv,
                device_id=device, device_id_type=MESH,
            )

        def at_line(steps):
            return {"ctx": (x * line + lax.rem(z + line + steps, line)) * 2 + core}

        def crew_peer(step):
            other = lax.rem(member + step, crew)
            spot = (other // 4) * line + pair * 2 + lax.rem(other, 2)
            return other, {"ctx": spot * 2 + lax.rem(other // 2, 2)}

        arrays = (
            (hk_in, hk), (hv_in, hv), (taps_in, taps), (seg_in, seg), (hq_in, hq), (ho_in, ho),
            (gain_in, gain),
        )
        loads = [
            pltpu.make_async_copy(src, dst, load_sem.at[place])
            for place, (src, dst) in enumerate(arrays)
        ]
        for head in range(heads):
            part = slice(head * HEAD_DIM, (head + 1) * HEAD_DIM)
            for src, dst in (
                (ak_in, kv.at[head, 2, 0]), (av_in, kv.at[head, 2, 1]),
                (aq_in, qc.at[head, 0]), (ao_in, qc.at[head, 1]),
            ):
                loads.append(pltpu.make_async_copy(src.at[:, part], dst, load_sem.at[len(loads)]))
        hk_load, hv_load, taps_load, seg_load, hq_load, ho_load, gain_load = loads[:7]
        head_loads = [loads[7 + 4 * head : 11 + 4 * head] for head in range(heads)]
        hk_load.start()
        hv_load.start()

        def at_x(steps):
            wide = crew // 4
            return {"ctx": (lax.rem(x + wide + steps, wide) * line + z) * 2 + core}

        def at_mp(steps):
            return {"mp": lax.rem(j + m + steps, m)}

        beside = [{"ctx": sibling}, at_line(1), at_line(-1)]
        if crew > 4:
            beside += [at_x(1), at_x(-1)]
        across = [at_mp(1), at_mp(-1)] if m > 1 else []
        greeted = beside + across + [{"ctx": one} for one in (after, before, ahead, behind)]
        rounds = [
            beside + across,
            beside + [at_line(2), at_line(-2)],
            [{"ctx": sibling}, at_line(4), at_line(-4)],
        ]
        barrier = pltpu.get_barrier_semaphore()
        for device in greeted:
            pl.semaphore_signal(barrier, inc=1, device_id=device, device_id_type=MESH)

        def tell(place):
            for device in rounds[place]:
                pl.semaphore_signal(token.at[place], inc=1, device_id=device, device_id_type=MESH)

        def hear(place):
            pl.semaphore_wait(token.at[place], len(rounds[place]))

        for load in (*head_loads[0], *head_loads[1]):
            load.start()
        stores = [
            pltpu.make_async_copy(src, dst, store_sem.at[place])
            for place, (src, dst) in enumerate((
                (daq, daq_out), (dak, dak_out), (dav, dav_out), (dhq, dhq_out), (dhk, dhk_out),
                (dhv, dhv_out), (fd, dfilter_out),
            ))
        ]


        hk_load.wait()
        hv_load.wait()
        product = hk[...].astype(F32) * hv[...].astype(F32)
        ext[ROWS:, :] = product
        for half in range(2):
            part = slice(half * width // 2, (half + 1) * width // 2)
            halo_out[half] = product[:, part].astype(BF16)

        pl.semaphore_wait(barrier, len(greeted))

        def halo_copy(half):
            return copy(
                halo_out.at[half], halo_in.at[half], one_send.at[half], one_recv.at[half],
                {"ctx": after},
            )

        halo_copy(0).start()
        halo_copy(1).start()
        for load in (seg_load, taps_load, *loads[15:], hq_load, ho_load, gain_load):
            load.start()

        def give_back(head):
            return copy(
                kv.at[head, 2], kv.at[head, 0], kv_send.at[head, 0], kv_recv.at[head, 0],
                {"ctx": behind},
            )

        def give_queries(head):
            return copy(
                qc.at[head], qc_in.at[head], kv_send.at[head, 1], kv_recv.at[head, 1],
                {"ctx": behind},
            )

        def give_on(head):
            return copy(
                kv.at[head, 2], kv.at[head, 4], kv_send.at[head, 2], kv_recv.at[head, 2],
                {"ctx": ahead},
            )

        def near_copy(head):
            return copy(
                kv.at[head, 2 * core], kv.at[head, 1], kv_send.at[head, 3], kv_recv.at[head, 3],
                {"ctx": sibling},
            )

        def far_copy(head):
            return copy(
                kv.at[head, 2 * core + 2], kv.at[head, 3], kv_send.at[head, 4],
                kv_recv.at[head, 4], {"ctx": sibling},
            )

        def send_back(head):
            for load in head_loads[head]:
                load.wait()
            give_back(head).start()
            give_queries(head).start()

        send_back(0)

        tell(0)

        def service(head):
            give_back(head).wait_recv()
            give_on(head).wait_recv()
            near_copy(head).start()
            far_copy(head).start()

        seg_load.wait()
        segrows[...] = jnp.zeros_like(segrows)
        asked = lax.rem(i + 2, n)
        spots = [asked - back_by for back_by in range(SPAN, -1, -1)] + [i - 1, i, i + 1]
        for row, block in enumerate(spots):
            inside = (block >= 0) & (block < n)
            held = seg[pl.ds(jnp.clip(block, 0, n - 1), 1), :]
            outside = -2 if row == SPAN + 3 else -1
            segrows[row : row + 1, :] = jnp.where(inside, held, outside).astype(F32)
        turned = segrows[...].T
        for place in range(3):
            row = SPAN + 1 + place
            segcols[place * ROWS : (place + 1) * ROWS, :] = jnp.broadcast_to(
                turned[:, row : row + 1], (ROWS, LANES)
            )

        query_seg = segrows[SPAN : SPAN + 1, :]
        key_at = lax.broadcasted_iota(jnp.int32, (ROWS, ROWS), 0)
        query_at = lax.broadcasted_iota(jnp.int32, (ROWS, ROWS), 1)
        for back_by in range(SPAN + 1):
            row = SPAN - back_by
            allowed = turned[:, row : row + 1] == query_seg
            if back_by == 0:
                allowed = allowed & (key_at <= query_at)
            bias[back_by * ROWS : (back_by + 1) * ROWS, :] = jnp.where(allowed, 0.0, FAR)

        def shift_rows(start, stop, begin, end):
            @pl.loop(begin, end)
            def _(column):
                part = lanes(column)
                for r in range(GROUP):
                    same = segcols[start - r : stop - r, :] == segcols[start:stop, :]
                    shifts[r, start:stop, part] = jnp.where(
                        same, ext[start - r : stop - r, part], 0.0
                    )

        shift_rows(ROWS + GROUP, 2 * ROWS, 0, columns)
        taps_load.wait()
        taps_t[...] = taps[...].T
        squares[...] = jnp.zeros_like(squares)
        crossed[...] = jnp.zeros_like(crossed)
        def tap_groups(column, piece, start, stop, total):
            part = lanes(column)
            own = segcols[ROWS + piece * PART : ROWS + (piece + 1) * PART, :]
            span = PART + GROUP * (QUAD - 1)

            def step(quad, total):
                first = pl.multiple_of(
                    ROWS + piece * PART - GROUP * (QUAD * quad + QUAD - 1), GROUP
                )
                begin = pl.multiple_of(GROUP * QUAD * quad, GROUP * QUAD)
                coeff = taps_t[pl.ds(begin, GROUP * QUAD), part]
                segs = segcols[pl.ds(first, span), :]
                terms = [None] * QUAD
                for r in range(GROUP):
                    block = shifts[r, pl.ds(first, span), part]
                    for k in range(QUAD):
                        off = GROUP * (QUAD - 1 - k)
                        at = GROUP * k + r
                        term = coeff[at : at + 1] * block[off : off + PART]
                        terms[k] = term if r == 0 else terms[k] + term
                for k in range(QUAD):
                    off = GROUP * (QUAD - 1 - k)
                    total = total + jnp.where(segs[off : off + PART] == own, terms[k], 0.0)
                return total

            return lax.fori_loop(start, stop, step, total)

        def convolve(column):
            part = lanes(column)
            for piece in range(pieces):
                rows = slice(piece * PART, (piece + 1) * PART)
                if piece == 0:
                    begun = jnp.zeros((PART, LANES), F32)
                else:
                    begun = mixed[rows, part]
                found = tap_groups(column, piece, inner[piece], quads, begun)
                mixed[rows, part] = found
                gate = hq[rows, part].astype(F32) * found
                heavy = gain[:, part] * ho[rows, part].astype(F32)
                gated[rows, part] = gate
                weighted[rows, part] = heavy
                squares[rows, :] += gate * gate
                crossed[rows, :] += heavy * gate

        def attend(head):
            near_copy(head).wait_recv()
            far_copy(head).wait_recv()
            give_queries(head).wait_recv()
            query, cot = qc_in[head, 0], qc_in[head, 1]
            key_all = kv[head, :, 0].reshape(keys, HEAD_DIM)
            value_all = kv[head, :, 1].reshape(keys, HEAD_DIM)
            scores = contract(key_all, query, 1, 1) * scale + bias[...]
            peak = jnp.max(scores, axis=0, keepdims=True)
            powers = jnp.exp(scores - peak)
            probs = powers * (1.0 / jnp.sum(powers, axis=0, keepdims=True))
            low = probs.astype(BF16)
            slope = contract(value_all, cot, 1, 1)
            offset = jnp.sum(low.astype(F32) * slope, axis=0, keepdims=True)
            score_grad = (probs * (slope - offset)).astype(BF16)
            dq_out[head] = (contract(score_grad, key_all, 0, 0) * scale).astype(BF16)
            grads[head, 0] = contract(score_grad, query, 1, 0) * scale
            grads[head, 1] = contract(low, cot, 1, 0)
            for place in range(2):
                rows = slice((2 * place + 1) * ROWS, (2 * place + 2) * ROWS)
                gs_out[head, place] = grads[head, :, rows].astype(BF16)
            gs_copy(head).start()

        def gs_copy(head):
            return copy(
                gs_out.at[head], gs_in.at[head], g_send.at[head, 0], g_recv.at[head, 0],
                {"ctx": sibling},
            )

        def dq_copy(head):
            return copy(
                dq_out.at[head], dq_in.at[head], g_send.at[head, 1], g_recv.at[head, 1],
                {"ctx": ahead},
            )

        def up_copy(head):
            return copy(
                up_out.at[head], up_in.at[head], g_send.at[head, 2], g_recv.at[head, 2],
                {"ctx": ahead},
            )

        def down_copy(head):
            return copy(
                down_out.at[head], down_in.at[head], g_send.at[head, 3], g_recv.at[head, 3],
                {"ctx": behind},
            )

        first_core = core == 0

        def give_grads(head):
            gs_copy(head).wait_recv()
            near = gs_in[head, 0].astype(F32)
            far = gs_in[head, 1].astype(F32)
            ours = grads[head, :, 0:ROWS]
            up_out[head] = (ours + jnp.where(first_core, near, 0.0)).astype(BF16)
            up_copy(head).start()
            ours = grads[head, :, 4 * ROWS : 5 * ROWS]
            down_out[head] = (ours + jnp.where(first_core, 0.0, far)).astype(BF16)
            down_copy(head).start()
            dq_copy(head).start()

        def take_grads(head):
            part = slice(head * HEAD_DIM, (head + 1) * HEAD_DIM)
            ours = grads[head, :, 2 * ROWS : 3 * ROWS]
            theirs = jnp.where(first_core, gs_in[head, 1].astype(F32), gs_in[head, 0].astype(F32))
            down_copy(head).wait_recv()
            up_copy(head).wait_recv()
            dq_copy(head).wait_recv()
            done = ours + theirs + up_in[head].astype(F32) + down_in[head].astype(F32)
            daq[:, part] = dq_in[head]
            dak[:, part] = done[0].astype(BF16)
            dav[:, part] = done[1].astype(BF16)

        @pl.loop(0, columns)
        def _(column):
            for piece in range(1, pieces):
                rows = slice(piece * PART, (piece + 1) * PART)
                mixed[rows, lanes(column)] = tap_groups(
                    column, piece, 0, inner[piece], jnp.zeros((PART, LANES), F32)
                )

        for load in (hq_load, ho_load, gain_load):
            load.wait()
        give_on(0).start()
        send_back(1)
        hear(0)
        tell(1)

        for half in range(2):
            part = slice(half * width // 2, (half + 1) * width // 2)
            halo_copy(half).wait_recv()
            if half == 0:
                give_on(1).start()
            else:
                send_back(2)
                give_on(2).start()
            ext[:ROWS, part] = halo_in[half].astype(F32)
            begin, end = half * columns // 2, (half + 1) * columns // 2
            shift_rows(GROUP, ROWS + GROUP, begin, end)

            @pl.loop(begin, end)
            def _(column):
                convolve(column)

        square_sum = jnp.sum(squares[...], axis=1, keepdims=True)
        cross_sum = jnp.sum(crossed[...], axis=1, keepdims=True)
        lane_at = lax.broadcasted_iota(jnp.int32, (ROWS, LANES), 1)
        squares[...] = jnp.where(lane_at == 0, square_sum, jnp.where(lane_at == 1, cross_sum, 0.0))
        sums[...] = squares[...].T[0:8]

        def sum_copy(step):
            return copy(
                sums, sums_in.at[step - 1], mp_send.at[step - 1], mp_recv.at[step - 1],
                {"mp": lax.rem(j + step, m)},
            )

        for step in range(1, m):
            sum_copy(step).start()

        hear(1)
        tell(2)
        send_back(3)
        give_on(3).start()
        service(0)
        attend(0)
        for step in range(1, m):
            sum_copy(step).wait_recv()
        whole = sums[...]
        for step in range(1, m):
            whole = whole + sums_in[step - 1]
        inverse = lax.rsqrt(whole[0:1] / channels + 1e-06)
        factor = inverse * inverse * inverse * (whole[1:2] / channels)
        squares[0:1, :] = inverse
        squares[1:2, :] = factor
        upright = squares[...].T
        squares[...] = jnp.broadcast_to(upright[:, 0:1], (ROWS, LANES))
        crossed[...] = jnp.broadcast_to(upright[:, 1:2], (ROWS, LANES))

        @pl.loop(0, columns)
        def _(column):
            part = lanes(column)
            slope = squares[...] * weighted[:, part] - gated[:, part] * crossed[...]
            dhq[:, part] = (slope * mixed[:, part]).astype(BF16)
            signal = slope * hq[:, part].astype(F32)
            sig[:ROWS, part] = signal
            sig_out[:, part] = signal.astype(BF16)

        sig_copy = copy(sig_out, sig_in, one_send.at[2], one_recv.at[2], {"ctx": before})
        sig_copy.start()
        stores[3].start()
        def correlate(quad):
            row = lax.broadcasted_iota(jnp.int32, (GROUP, LANES), 0)
            span = PART + GROUP * (QUAD - 1)

            @pl.loop(0, columns)
            def _(column):
                part = lanes(column)
                for piece in range(pieces):
                    rows = slice(piece * PART, (piece + 1) * PART)
                    own = segcols[ROWS + piece * PART : ROWS + (piece + 1) * PART, :]
                    signal = sig[rows, part]
                    first = ROWS + piece * PART - GROUP * (QUAD * quad + QUAD - 1)
                    segs = segcols[first : first + span, :]
                    masked = [
                        jnp.where(segs[off : off + PART] == own, signal, 0.0)
                        for off in range(GROUP * (QUAD - 1), -1, -GROUP)
                    ]
                    found = [[] for _ in range(QUAD)]
                    for r in range(GROUP):
                        block = shifts[r, first : first + span, part]
                        for k in range(QUAD):
                            off = GROUP * (QUAD - 1 - k)
                            term = masked[k] * block[off : off + PART]
                            found[k].append(term.reshape(PART // 8, 8, LANES).sum(axis=0))
                    for k in range(QUAD):
                        begin = GROUP * (QUAD * quad + k)
                        total = fold(found[k], row)
                        if piece:
                            total = total + ft[begin : begin + GROUP, part]
                        ft[begin : begin + GROUP, part] = total

        def fa_copy(chunk, step):
            other, device = crew_peer(step)
            return copy(
                fa_out.at[chunk, other], fa_in.at[chunk, step - 1], f_send.at[0, chunk],
                f_recv.at[0, chunk], device,
            )

        def fb_copy(chunk, step):
            return copy(
                fb.at[chunk, pair], fb.at[chunk, pair], f_send.at[1, chunk],
                f_recv.at[1, chunk], at_line(2 * step),
            )

        def fd_copy(chunk, step):
            _, device = crew_peer(step)
            return copy(
                fd.at[chunk, member], fd.at[chunk, member], f_send.at[2, chunk],
                f_recv.at[2, chunk], device,
            )

        def wait_bytes(held, sems, phase, chunk, count):
            ref = held.at[chunk, pl.ds(0, count)]
            pltpu.make_async_copy(ref, ref, sems.at[phase, chunk]).wait()

        def filter_out(quad):
            owned = GROUP * QUAD // crew_taps
            for owner in range(quad * owned, (quad + 1) * owned):
                rows = slice(owner * crew_taps, (owner + 1) * crew_taps)
                tile = [ft[rows, lanes(side)] for side in range(sides)]
                fa_out[0, owner] = jnp.concatenate(tile).astype(BF16)
                step = lax.rem(owner - member + crew, crew)

                @pl.when(step != 0)
                def _():
                    fa_copy(0, step).start()

        def filter_sum(chunk):
            wait_bytes(fa_in, f_recv, 0, chunk, crew - 1)
            rows = pl.ds(pl.multiple_of(member * crew_taps, crew_taps), crew_taps)
            tile = [ft[rows, lanes(sides * chunk + side)] for side in range(sides)]
            total = jnp.concatenate(tile)
            for step in range(1, crew):
                total = total + fa_in[chunk, step - 1].astype(F32)
            fb[chunk, pair] = total.astype(BF16)
            for step in sorted(range(1, pairs), key=lambda step: -min(step, pairs - step)):
                fb_copy(chunk, step).start()

        def filter_whole(chunk):
            wait_bytes(fb, f_recv, 1, chunk, pairs - 1)
            total = fb[chunk, 0].astype(F32)
            for place in range(1, pairs):
                total = total + fb[chunk, place].astype(F32)
            fd[chunk, member] = (total * (n * ROWS) ** (-0.5)).astype(BF16)
            for step in sorted(range(1, crew), key=lambda step: -min(step, crew - step)):
                fd_copy(chunk, step).start()

        def filter_done(chunk):
            wait_bytes(fd, f_recv, 2, chunk, crew - 1)

        def spread(column):
            part = lanes(column)
            reach = 2 * ROWS - GROUP
            for r in range(GROUP):
                same = segcols[ROWS + r : ROWS + r + reach, :] == segcols[ROWS : ROWS + reach, :]
                back[r] = jnp.where(same, sig[r : r + reach, part], 0.0)
            for piece in range(ROWS // PART):
                rows = slice(piece * PART, (piece + 1) * PART)
                own = segcols[ROWS + piece * PART : ROWS + (piece + 1) * PART, :]
                span = PART + GROUP * (QUAD - 1)

                def step(quad, total):
                    begin = pl.multiple_of(GROUP * QUAD * quad, GROUP * QUAD)
                    first = pl.multiple_of(piece * PART + begin, GROUP)
                    coeff = taps_t[pl.ds(begin, GROUP * QUAD), part]
                    segs = segcols[pl.ds(pl.multiple_of(ROWS + first, GROUP), span), :]
                    terms = [None] * QUAD
                    for r in range(GROUP):
                        block = back[r, pl.ds(first, span), :]
                        for k in range(QUAD):
                            at = GROUP * k + r
                            term = coeff[at : at + 1] * block[GROUP * k : GROUP * k + PART]
                            terms[k] = term if r == 0 else terms[k] + term
                    for k in range(QUAD):
                        same = segs[GROUP * k : GROUP * k + PART] == own
                        total = total + jnp.where(same, terms[k], 0.0)
                    return total

                found = lax.fori_loop(
                    0, TAPS // GROUP // QUAD, step, jnp.zeros((PART, LANES), F32)
                )
                dhk[rows, part] = (found * hv[rows, part].astype(F32)).astype(BF16)
                dhv[rows, part] = (found * hk[rows, part].astype(F32)).astype(BF16)

        correlate(0)
        hear(2)
        filter_out(0)
        give_grads(0)
        service(1)
        correlate(1)
        filter_out(1)
        service(2)
        correlate(2)
        filter_out(2)
        correlate(3)
        filter_out(3)
        attend(1)
        service(3)
        attend(2)
        give_grads(1)
        attend(3)
        filter_sum(0)
        give_grads(2)
        give_grads(3)
        sig_copy.wait_recv()
        sig[ROWS:, :] = sig_in[...].astype(F32)
        spread(0)
        spread(1)
        spread(2)
        spread(3)
        stores[4].start()
        stores[5].start()
        take_grads(0)
        filter_whole(0)
        take_grads(1)
        take_grads(2)
        take_grads(3)
        for place in range(3):
            stores[place].start()

        halo_copy(0).wait_send()
        halo_copy(1).wait_send()
        sig_copy.wait_send()
        for step in range(1, m):
            sum_copy(step).wait_send()
        for head in range(heads):
            for made in (
                give_back, give_queries, give_on, near_copy, far_copy, gs_copy, dq_copy, up_copy,
                down_copy,
            ):
                made(head).wait_send()
        for chunk in range(chunks):
            wait_bytes(fa_in, f_send, 0, chunk, crew - 1)
            wait_bytes(fb, f_send, 1, chunk, pairs - 1)
        for chunk in range(chunks):
            filter_done(chunk)
        stores[6].start()
        for chunk in range(chunks):
            wait_bytes(fd, f_send, 2, chunk, crew - 1)
        for store in stores:
            store.wait()

    vmem = pltpu.VMEM
    dma = pltpu.SemaphoreType.DMA
    square = (ROWS, LANES)
    wide = vmem((ROWS, width), BF16)
    scratch = [
        wide, wide, wide, wide, wide, wide,
        wide, wide, wide, wide,
        vmem((width, TAPS), F32),
        vmem((1, width), F32),
        vmem((n, ROWS), jnp.int32),
        vmem((ROWS, LANES), F32),
        vmem((3 * ROWS, LANES), F32),
        vmem((keys, ROWS), F32),
        vmem((TAPS, width), F32),
        vmem((2 * ROWS, width), F32),
        vmem((2, ROWS, width // 2), BF16),
        vmem((2, ROWS, width // 2), BF16),
        vmem((GROUP, 2 * ROWS, width), F32),
        vmem((ROWS, width), F32),
        vmem((ROWS, width), F32),
        vmem((ROWS, width), F32),
        vmem(square, F32),
        vmem(square, F32),
        vmem((8, ROWS), F32),
        vmem((max(1, m - 1), 8, ROWS), F32),
        vmem((2 * ROWS, width), F32),
        wide,
        wide,
        vmem((GROUP, 2 * ROWS - GROUP, LANES), F32),
        vmem((TAPS, width), F32),
        vmem((chunks, crew, sides * crew_taps, LANES), BF16),
        vmem((chunks, crew - 1, sides * crew_taps, LANES), BF16),
        vmem((chunks, pairs, sides * crew_taps, LANES), BF16),
        vmem((chunks, crew, sides * crew_taps, LANES), BF16),
        vmem((heads, SPAN + 1, 2, ROWS, HEAD_DIM), BF16),
        vmem((heads, 2, ROWS, HEAD_DIM), BF16),
        vmem((heads, 2, ROWS, HEAD_DIM), BF16),
        vmem((heads, ROWS, HEAD_DIM), BF16),
        vmem((heads, ROWS, HEAD_DIM), BF16),
        vmem((heads, 2, keys, HEAD_DIM), F32),
        vmem((heads, 2, 2, ROWS, HEAD_DIM), BF16),
        vmem((heads, 2, 2, ROWS, HEAD_DIM), BF16),
        vmem((heads, 2, ROWS, HEAD_DIM), BF16),
        vmem((heads, 2, ROWS, HEAD_DIM), BF16),
        vmem((heads, 2, ROWS, HEAD_DIM), BF16),
        vmem((heads, 2, ROWS, HEAD_DIM), BF16),
        dma((7 + 4 * heads,)),
        dma((3,)),
        dma((3,)),
        dma((max(1, m - 1),)),
        dma((max(1, m - 1),)),
        dma((heads, 5)),
        dma((heads, 5)),
        dma((heads, 4)),
        dma((heads, 4)),
        dma((3, chunks)),
        dma((3, chunks)),
        pltpu.SemaphoreType.REGULAR((3,)),
        dma((7,)),
    ]
    return kernel, scratch, (chunks, crew, sides * crew_taps, LANES)


def write_out(*refs):
    sources, results, held, (dfilter, sems) = refs[:7], refs[7:14], refs[14:21], refs[21:]
    loads = [
        pltpu.make_async_copy(src, mid, sems.at[0, place])
        for place, (src, mid) in enumerate(zip(sources, held))
    ]
    stores = [
        pltpu.make_async_copy(mid, dst, sems.at[1, place])
        for place, (mid, dst) in enumerate(zip((*held[:6], dfilter), results))
    ]
    for load in reversed(loads):
        load.start()
    loads[6].wait()
    fd = held[6]
    chunks, crew, rows, _ = fd.shape
    taps = TAPS // crew
    sides = rows // taps
    for chunk in range(chunks):
        for side in range(sides):
            tap_rows = fd[chunk, :, side * taps : (side + 1) * taps].astype(F32)
            begin = (sides * chunk + side) * LANES
            dfilter[begin : begin + LANES, :] = tap_rows.reshape(TAPS, LANES).T
    stores[6].start()
    for load, store in zip(loads[:6], stores[:6]):
        load.wait()
        store.start()
    for store in stores:
        store.wait()


def build(mesh, line):
    n, m = mesh.shape["ctx"], mesh.shape["mp"]

    def body(aq, ak, av, ao, hq, hk, hv, ho, taps, gain, seg):
        rows, width = aq.shape
        kernel, scratch, rows_shape = make_kernel(n, m, width, line)
        wide = jax.ShapeDtypeStruct((rows, width), BF16)
        shapes = (wide,) * 6 + (jax.ShapeDtypeStruct((width, TAPS), F32),)
        found_shapes = (wide,) * 6 + (jax.ShapeDtypeStruct(rows_shape, BF16),)
        far = pl.BlockSpec(memory_space=pltpu.HBM)
        found = pl.pallas_call(
            kernel,
            out_shape=found_shapes,
            in_specs=[far] * 11,
            out_specs=(far,) * 7,
            scratch_shapes=scratch,
            compiler_params=pltpu.CompilerParams(
                collective_id=0, has_side_effects=True, vmem_limit_bytes=60 * 2**20
            ),
        )(aq, ak, av, ao, hq, hk, hv, ho, taps, gain.reshape(1, width), seg.reshape(n, rows))
        return pl.pallas_call(
            write_out,
            out_shape=shapes,
            in_specs=[far] * 7,
            out_specs=(far,) * 7,
            scratch_shapes=[pltpu.VMEM(one.shape, one.dtype) for one in found_shapes]
            + [pltpu.VMEM((width, TAPS), F32), pltpu.SemaphoreType.DMA((2, 7))],
            compiler_params=pltpu.CompilerParams(vmem_limit_bytes=60 * 2**20),
        )(*found)

    wide = P("ctx", "mp")
    return jax.shard_map(
        body,
        mesh=mesh,
        in_specs=(wide,) * 8 + (P("mp", None), P("mp"), P()),
        out_specs=(wide,) * 6 + (P("mp", None),),
        check_vma=False,
    )


def solution(mesh):
    return build(mesh, LINE)
```

```python
import jax
import jax.numpy as jnp
from jax import lax
from jax.experimental import pallas as pl
from jax.experimental.pallas import tpu as pltpu
from jax.sharding import PartitionSpec as P

SPAN = 4
HEAD_DIM = 128
TAPS = 128
ROWS = 128
LINE = 16
GROUP = 8
QUAD = 4
PART = 64
LANES = 128
F32 = jnp.float32
BF16 = jnp.bfloat16
FAR = -1e30
MESH = pl.DeviceIdType.MESH


def contract(left, right, left_dim, right_dim):
    return lax.dot_general(
        left, right, (((left_dim,), (right_dim,)), ((), ())), preferred_element_type=F32
    )


def fold(tiles, row):
    for bit in (4, 2, 1):
        low = (row & bit) == 0
        half = len(tiles) // 2
        folded = []
        for first, second in zip(tiles[:half], tiles[half:]):
            keep = jnp.where(low, first, second)
            move = jnp.where(low, second, first)
            up = pltpu.roll(move, 8 - bit, 0)
            folded.append(keep + (up if bit == 4 else jnp.where(low, up, pltpu.roll(move, bit, 0))))
        tiles = folded
    return tiles[0]


def make_kernel(n, m, width, line):
    heads = width // HEAD_DIM
    columns = width // LANES
    channels = width * m
    pairs = line // 2
    crew = 2 * n // line
    crew_taps = TAPS // crew
    chunks = 1
    sides = columns // chunks
    keys = (SPAN + 1) * ROWS
    scale = HEAD_DIM ** (-0.5)
    pieces = ROWS // PART
    quads = TAPS // GROUP // QUAD
    inner = [piece * PART // (GROUP * QUAD) if piece else 0 for piece in range(pieces)]

    def lanes(index):
        return pl.ds(pl.multiple_of(index * LANES, LANES), LANES)

    def kernel(
        aq_in, ak_in, av_in, ao_in, hq_in, hk_in, hv_in, ho_in, taps_in, gain_in, seg_in,
        daq_out, dak_out, dav_out, dhq_out, dhk_out, dhv_out, dfilter_out,
        daq, dak, dav, dhq, dhk, dhv,
        hq, hk, hv, ho, taps, gain, seg,
        segrows, segcols, bias, taps_t, ext, halo_out, halo_in, shifts,
        mixed, gated, weighted, squares, crossed, sums, sums_in,
        sig, sig_out, sig_in, back, ft, fa_out, fa_in, fb, fd,
        kv, qc, qc_in, dq_out, dq_in, grads, gs_out, gs_in, up_out, up_in, down_out, down_in,
        load_sem, one_send, one_recv, mp_send, mp_recv, kv_send, kv_recv,
        g_send, g_recv, f_send, f_recv, token, store_sem,
    ):
        i = lax.axis_index("ctx")
        j = lax.axis_index("mp")
        core = lax.rem(i, 2)
        chip = i // 2
        z = lax.rem(chip, line)
        x = chip // line
        pair = z // 2
        member = (x * 2 + core) * 2 + lax.rem(z, 2)
        after, before = lax.rem(i + 1, n), lax.rem(i + n - 1, n)
        ahead, behind = lax.rem(i + 2, n), lax.rem(i + n - 2, n)
        sibling = i + 1 - 2 * core

        def copy(src, dst, send, recv, device):
            return pltpu.make_async_remote_copy(
                src_ref=src, dst_ref=dst, send_sem=send, recv_sem=recv,
                device_id=device, device_id_type=MESH,
            )

        def at_line(steps):
            return {"ctx": (x * line + lax.rem(z + line + steps, line)) * 2 + core}

        def crew_peer(step):
            other = lax.rem(member + step, crew)
            spot = (other // 4) * line + pair * 2 + lax.rem(other, 2)
            return other, {"ctx": spot * 2 + lax.rem(other // 2, 2)}

        arrays = (
            (hk_in, hk), (hv_in, hv), (taps_in, taps), (seg_in, seg), (hq_in, hq), (ho_in, ho),
            (gain_in, gain),
        )
        loads = [
            pltpu.make_async_copy(src, dst, load_sem.at[place])
            for place, (src, dst) in enumerate(arrays)
        ]
        for head in range(heads):
            part = slice(head * HEAD_DIM, (head + 1) * HEAD_DIM)
            for src, dst in (
                (ak_in, kv.at[head, 2, 0]), (av_in, kv.at[head, 2, 1]),
                (aq_in, qc.at[head, 0]), (ao_in, qc.at[head, 1]),
            ):
                loads.append(pltpu.make_async_copy(src.at[:, part], dst, load_sem.at[len(loads)]))
        hk_load, hv_load, taps_load, seg_load, hq_load, ho_load, gain_load = loads[:7]
        head_loads = [loads[7 + 4 * head : 11 + 4 * head] for head in range(heads)]
        hk_load.start()
        hv_load.start()

        def at_x(steps):
            wide = crew // 4
            return {"ctx": (lax.rem(x + wide + steps, wide) * line + z) * 2 + core}

        def at_mp(steps):
            return {"mp": lax.rem(j + m + steps, m)}

        beside = [{"ctx": sibling}, at_line(1), at_line(-1)]
        if crew > 4:
            beside += [at_x(1), at_x(-1)]
        across = [at_mp(1), at_mp(-1)] if m > 1 else []
        greeted = beside + across + [{"ctx": one} for one in (after, before, ahead, behind)]
        rounds = [
            beside + across,
            beside + [at_line(2), at_line(-2)],
            [{"ctx": sibling}, at_line(4), at_line(-4)],
        ]
        barrier = pltpu.get_barrier_semaphore()
        for device in greeted:
            pl.semaphore_signal(barrier, inc=1, device_id=device, device_id_type=MESH)

        def tell(place):
            for device in rounds[place]:
                pl.semaphore_signal(token.at[place], inc=1, device_id=device, device_id_type=MESH)

        def hear(place):
            pl.semaphore_wait(token.at[place], len(rounds[place]))

        for load in (*head_loads[0], *head_loads[1]):
            load.start()
        stores = [
            pltpu.make_async_copy(src, dst, store_sem.at[place])
            for place, (src, dst) in enumerate((
                (daq, daq_out), (dak, dak_out), (dav, dav_out), (dhq, dhq_out), (dhk, dhk_out),
                (dhv, dhv_out), (fd, dfilter_out),
            ))
        ]


        hk_load.wait()
        hv_load.wait()
        product = hk[...].astype(F32) * hv[...].astype(F32)
        ext[ROWS:, :] = product
        for half in range(2):
            part = slice(half * width // 2, (half + 1) * width // 2)
            halo_out[half] = product[:, part].astype(BF16)

        pl.semaphore_wait(barrier, len(greeted))

        def halo_copy(half):
            return copy(
                halo_out.at[half], halo_in.at[half], one_send.at[half], one_recv.at[half],
                {"ctx": after},
            )

        halo_copy(0).start()
        halo_copy(1).start()
        for load in (seg_load, taps_load, *loads[15:], hq_load, ho_load, gain_load):
            load.start()

        def give_back(head):
            return copy(
                kv.at[head, 2], kv.at[head, 0], kv_send.at[head, 0], kv_recv.at[head, 0],
                {"ctx": behind},
            )

        def give_queries(head):
            return copy(
                qc.at[head], qc_in.at[head], kv_send.at[head, 1], kv_recv.at[head, 1],
                {"ctx": behind},
            )

        def give_on(head):
            return copy(
                kv.at[head, 2], kv.at[head, 4], kv_send.at[head, 2], kv_recv.at[head, 2],
                {"ctx": ahead},
            )

        def near_copy(head):
            return copy(
                kv.at[head, 2 * core], kv.at[head, 1], kv_send.at[head, 3], kv_recv.at[head, 3],
                {"ctx": sibling},
            )

        def far_copy(head):
            return copy(
                kv.at[head, 2 * core + 2], kv.at[head, 3], kv_send.at[head, 4],
                kv_recv.at[head, 4], {"ctx": sibling},
            )

        def send_back(head):
            for load in head_loads[head]:
                load.wait()
            give_back(head).start()
            give_queries(head).start()

        send_back(0)

        tell(0)

        def service(head):
            give_back(head).wait_recv()
            give_on(head).wait_recv()
            near_copy(head).start()
            far_copy(head).start()

        seg_load.wait()
        segrows[...] = jnp.zeros_like(segrows)
        asked = lax.rem(i + 2, n)
        spots = [asked - back_by for back_by in range(SPAN, -1, -1)] + [i - 1, i, i + 1]
        for row, block in enumerate(spots):
            inside = (block >= 0) & (block < n)
            held = seg[pl.ds(jnp.clip(block, 0, n - 1), 1), :]
            outside = -2 if row == SPAN + 3 else -1
            segrows[row : row + 1, :] = jnp.where(inside, held, outside).astype(F32)
        turned = segrows[...].T
        for place in range(3):
            row = SPAN + 1 + place
            segcols[place * ROWS : (place + 1) * ROWS, :] = jnp.broadcast_to(
                turned[:, row : row + 1], (ROWS, LANES)
            )

        query_seg = segrows[SPAN : SPAN + 1, :]
        key_at = lax.broadcasted_iota(jnp.int32, (ROWS, ROWS), 0)
        query_at = lax.broadcasted_iota(jnp.int32, (ROWS, ROWS), 1)
        for back_by in range(SPAN + 1):
            row = SPAN - back_by
            allowed = turned[:, row : row + 1] == query_seg
            if back_by == 0:
                allowed = allowed & (key_at <= query_at)
            bias[back_by * ROWS : (back_by + 1) * ROWS, :] = jnp.where(allowed, 0.0, FAR)

        def shift_rows(start, stop, begin, end):
            for r in range(GROUP):
                same = segcols[start - r : stop - r, :] == segcols[start:stop, :]
                for column in range(begin, end):
                    part = slice(column * LANES, (column + 1) * LANES)
                    shifts[r, start:stop, part] = jnp.where(
                        same, ext[start - r : stop - r, part], 0.0
                    )

        shift_rows(ROWS + GROUP, 2 * ROWS, 0, columns)
        taps_load.wait()
        taps_t[...] = taps[...].T
        squares[...] = jnp.zeros_like(squares)
        crossed[...] = jnp.zeros_like(crossed)
        def tap_groups(column, piece, start, stop, total):
            part = lanes(column)
            own = segcols[ROWS + piece * PART : ROWS + (piece + 1) * PART, :]
            span = PART + GROUP * (QUAD - 1)

            def step(quad, total):
                first = pl.multiple_of(
                    ROWS + piece * PART - GROUP * (QUAD * quad + QUAD - 1), GROUP
                )
                begin = pl.multiple_of(GROUP * QUAD * quad, GROUP * QUAD)
                coeff = taps_t[pl.ds(begin, GROUP * QUAD), part]
                segs = segcols[pl.ds(first, span), :]
                terms = [None] * QUAD
                for r in range(GROUP):
                    block = shifts[r, pl.ds(first, span), part]
                    for k in range(QUAD):
                        off = GROUP * (QUAD - 1 - k)
                        at = GROUP * k + r
                        term = coeff[at : at + 1] * block[off : off + PART]
                        terms[k] = term if r == 0 else terms[k] + term
                for k in range(QUAD):
                    off = GROUP * (QUAD - 1 - k)
                    total = total + jnp.where(segs[off : off + PART] == own, terms[k], 0.0)
                return total

            return lax.fori_loop(start, stop, step, total)

        def convolve(column):
            part = lanes(column)
            for piece in range(pieces):
                rows = slice(piece * PART, (piece + 1) * PART)
                if piece == 0:
                    begun = jnp.zeros((PART, LANES), F32)
                else:
                    begun = mixed[rows, part]
                found = tap_groups(column, piece, inner[piece], quads, begun)
                mixed[rows, part] = found
                gate = hq[rows, part].astype(F32) * found
                heavy = gain[:, part] * ho[rows, part].astype(F32)
                gated[rows, part] = gate
                weighted[rows, part] = heavy
                squares[rows, :] += gate * gate
                crossed[rows, :] += heavy * gate

        def attend(head):
            near_copy(head).wait_recv()
            far_copy(head).wait_recv()
            give_queries(head).wait_recv()
            query, cot = qc_in[head, 0], qc_in[head, 1]
            key_all = kv[head, :, 0].reshape(keys, HEAD_DIM)
            value_all = kv[head, :, 1].reshape(keys, HEAD_DIM)
            scores = contract(key_all, query, 1, 1) * scale + bias[...]
            peak = jnp.max(scores, axis=0, keepdims=True)
            powers = jnp.exp(scores - peak)
            probs = powers * (1.0 / jnp.sum(powers, axis=0, keepdims=True))
            low = probs.astype(BF16)
            slope = contract(value_all, cot, 1, 1)
            offset = jnp.sum(low.astype(F32) * slope, axis=0, keepdims=True)
            score_grad = (probs * (slope - offset)).astype(BF16)
            dq_out[head] = (contract(score_grad, key_all, 0, 0) * scale).astype(BF16)
            grads[head, 0] = contract(score_grad, query, 1, 0) * scale
            grads[head, 1] = contract(low, cot, 1, 0)
            for place in range(2):
                rows = slice((2 * place + 1) * ROWS, (2 * place + 2) * ROWS)
                gs_out[head, place] = grads[head, :, rows].astype(BF16)
            gs_copy(head).start()

        def gs_copy(head):
            return copy(
                gs_out.at[head], gs_in.at[head], g_send.at[head, 0], g_recv.at[head, 0],
                {"ctx": sibling},
            )

        def dq_copy(head):
            return copy(
                dq_out.at[head], dq_in.at[head], g_send.at[head, 1], g_recv.at[head, 1],
                {"ctx": ahead},
            )

        def up_copy(head):
            return copy(
                up_out.at[head], up_in.at[head], g_send.at[head, 2], g_recv.at[head, 2],
                {"ctx": ahead},
            )

        def down_copy(head):
            return copy(
                down_out.at[head], down_in.at[head], g_send.at[head, 3], g_recv.at[head, 3],
                {"ctx": behind},
            )

        first_core = core == 0

        def give_grads(head):
            gs_copy(head).wait_recv()
            near = gs_in[head, 0].astype(F32)
            far = gs_in[head, 1].astype(F32)
            ours = grads[head, :, 0:ROWS]
            up_out[head] = (ours + jnp.where(first_core, near, 0.0)).astype(BF16)
            up_copy(head).start()
            ours = grads[head, :, 4 * ROWS : 5 * ROWS]
            down_out[head] = (ours + jnp.where(first_core, 0.0, far)).astype(BF16)
            down_copy(head).start()
            dq_copy(head).start()

        def take_grads(head):
            part = slice(head * HEAD_DIM, (head + 1) * HEAD_DIM)
            ours = grads[head, :, 2 * ROWS : 3 * ROWS]
            theirs = jnp.where(first_core, gs_in[head, 1].astype(F32), gs_in[head, 0].astype(F32))
            down_copy(head).wait_recv()
            up_copy(head).wait_recv()
            dq_copy(head).wait_recv()
            done = ours + theirs + up_in[head].astype(F32) + down_in[head].astype(F32)
            daq[:, part] = dq_in[head]
            dak[:, part] = done[0].astype(BF16)
            dav[:, part] = done[1].astype(BF16)

        @pl.loop(0, columns)
        def _(column):
            for piece in range(1, pieces):
                rows = slice(piece * PART, (piece + 1) * PART)
                mixed[rows, lanes(column)] = tap_groups(
                    column, piece, 0, inner[piece], jnp.zeros((PART, LANES), F32)
                )

        for load in (hq_load, ho_load, gain_load):
            load.wait()
        give_on(0).start()
        send_back(1)
        hear(0)
        tell(1)

        for half in range(2):
            part = slice(half * width // 2, (half + 1) * width // 2)
            halo_copy(half).wait_recv()
            if half == 0:
                give_on(1).start()
            else:
                send_back(2)
                give_on(2).start()
            ext[:ROWS, part] = halo_in[half].astype(F32)
            begin, end = half * columns // 2, (half + 1) * columns // 2
            shift_rows(GROUP, ROWS + GROUP, begin, end)

            @pl.loop(begin, end)
            def _(column):
                convolve(column)

        square_sum = jnp.sum(squares[...], axis=1, keepdims=True)
        cross_sum = jnp.sum(crossed[...], axis=1, keepdims=True)
        lane_at = lax.broadcasted_iota(jnp.int32, (ROWS, LANES), 1)
        squares[...] = jnp.where(lane_at == 0, square_sum, jnp.where(lane_at == 1, cross_sum, 0.0))
        sums[...] = squares[...].T[0:8]

        def sum_copy(step):
            return copy(
                sums, sums_in.at[step - 1], mp_send.at[step - 1], mp_recv.at[step - 1],
                {"mp": lax.rem(j + step, m)},
            )

        for step in range(1, m):
            sum_copy(step).start()

        hear(1)
        tell(2)
        send_back(3)
        give_on(3).start()
        service(0)
        attend(0)
        for step in range(1, m):
            sum_copy(step).wait_recv()
        whole = sums[...]
        for step in range(1, m):
            whole = whole + sums_in[step - 1]
        inverse = lax.rsqrt(whole[0:1] / channels + 1e-06)
        factor = inverse * inverse * inverse * (whole[1:2] / channels)
        squares[0:1, :] = inverse
        squares[1:2, :] = factor
        upright = squares[...].T
        squares[...] = jnp.broadcast_to(upright[:, 0:1], (ROWS, LANES))
        crossed[...] = jnp.broadcast_to(upright[:, 1:2], (ROWS, LANES))

        @pl.loop(0, columns)
        def _(column):
            part = lanes(column)
            slope = squares[...] * weighted[:, part] - gated[:, part] * crossed[...]
            signal = slope * hq[:, part].astype(F32)
            sig[:ROWS, part] = signal
            sig_out[:, part] = signal.astype(BF16)

        sig_copy = copy(sig_out, sig_in, one_send.at[2], one_recv.at[2], {"ctx": before})
        sig_copy.start()
        def correlate(quad):
            row = lax.broadcasted_iota(jnp.int32, (GROUP, LANES), 0)
            span = PART + GROUP * (QUAD - 1)

            @pl.loop(0, columns)
            def _(column):
                part = lanes(column)
                for piece in range(pieces):
                    rows = slice(piece * PART, (piece + 1) * PART)
                    own = segcols[ROWS + piece * PART : ROWS + (piece + 1) * PART, :]
                    signal = sig[rows, part]
                    first = ROWS + piece * PART - GROUP * (QUAD * quad + QUAD - 1)
                    segs = segcols[first : first + span, :]
                    masked = [
                        jnp.where(segs[off : off + PART] == own, signal, 0.0)
                        for off in range(GROUP * (QUAD - 1), -1, -GROUP)
                    ]
                    found = [[] for _ in range(QUAD)]
                    for r in range(GROUP):
                        block = shifts[r, first : first + span, part]
                        for k in range(QUAD):
                            off = GROUP * (QUAD - 1 - k)
                            term = masked[k] * block[off : off + PART]
                            found[k].append(term.reshape(PART // 8, 8, LANES).sum(axis=0))
                    for k in range(QUAD):
                        begin = GROUP * (QUAD * quad + k)
                        total = fold(found[k], row)
                        if piece:
                            total = total + ft[begin : begin + GROUP, part]
                        ft[begin : begin + GROUP, part] = total

        def fa_copy(chunk, step):
            other, device = crew_peer(step)
            return copy(
                fa_out.at[chunk, other], fa_in.at[chunk, step - 1], f_send.at[0, chunk],
                f_recv.at[0, chunk], device,
            )

        def fb_copy(chunk, step):
            return copy(
                fb.at[chunk, pair], fb.at[chunk, pair], f_send.at[1, chunk],
                f_recv.at[1, chunk], at_line(2 * step),
            )

        def fd_copy(chunk, step):
            _, device = crew_peer(step)
            return copy(
                fd.at[chunk, member], fd.at[chunk, member], f_send.at[2, chunk],
                f_recv.at[2, chunk], device,
            )

        def wait_bytes(held, sems, phase, chunk, count):
            ref = held.at[chunk, pl.ds(0, count)]
            pltpu.make_async_copy(ref, ref, sems.at[phase, chunk]).wait()

        def filter_out(quad):
            owned = GROUP * QUAD // crew_taps
            for owner in range(quad * owned, (quad + 1) * owned):
                rows = slice(owner * crew_taps, (owner + 1) * crew_taps)
                tile = [ft[rows, lanes(side)] for side in range(sides)]
                fa_out[0, owner] = jnp.concatenate(tile).astype(BF16)
                step = lax.rem(owner - member + crew, crew)

                @pl.when(step != 0)
                def _():
                    fa_copy(0, step).start()

        def filter_sum(chunk):
            wait_bytes(fa_in, f_recv, 0, chunk, crew - 1)
            rows = pl.ds(pl.multiple_of(member * crew_taps, crew_taps), crew_taps)
            tile = [ft[rows, lanes(sides * chunk + side)] for side in range(sides)]
            total = jnp.concatenate(tile)
            for step in range(1, crew):
                total = total + fa_in[chunk, step - 1].astype(F32)
            fb[chunk, pair] = total.astype(BF16)
            for step in sorted(range(1, pairs), key=lambda step: -min(step, pairs - step)):
                fb_copy(chunk, step).start()

        def filter_whole(chunk):
            wait_bytes(fb, f_recv, 1, chunk, pairs - 1)
            total = fb[chunk, 0].astype(F32)
            for place in range(1, pairs):
                total = total + fb[chunk, place].astype(F32)
            fd[chunk, member] = (total * (n * ROWS) ** (-0.5)).astype(BF16)
            for step in sorted(range(1, crew), key=lambda step: -min(step, crew - step)):
                fd_copy(chunk, step).start()

        def filter_done(chunk):
            wait_bytes(fd, f_recv, 2, chunk, crew - 1)

        def spread(column):
            part = lanes(column)
            reach = 2 * ROWS - GROUP
            for r in range(GROUP):
                same = segcols[ROWS + r : ROWS + r + reach, :] == segcols[ROWS : ROWS + reach, :]
                back[r] = jnp.where(same, sig[r : r + reach, part], 0.0)
            for piece in range(ROWS // PART):
                rows = slice(piece * PART, (piece + 1) * PART)
                own = segcols[ROWS + piece * PART : ROWS + (piece + 1) * PART, :]
                span = PART + GROUP * (QUAD - 1)

                def step(quad, total):
                    begin = pl.multiple_of(GROUP * QUAD * quad, GROUP * QUAD)
                    first = pl.multiple_of(piece * PART + begin, GROUP)
                    coeff = taps_t[pl.ds(begin, GROUP * QUAD), part]
                    segs = segcols[pl.ds(pl.multiple_of(ROWS + first, GROUP), span), :]
                    terms = [None] * QUAD
                    for r in range(GROUP):
                        block = back[r, pl.ds(first, span), :]
                        for k in range(QUAD):
                            at = GROUP * k + r
                            term = coeff[at : at + 1] * block[GROUP * k : GROUP * k + PART]
                            terms[k] = term if r == 0 else terms[k] + term
                    for k in range(QUAD):
                        same = segs[GROUP * k : GROUP * k + PART] == own
                        total = total + jnp.where(same, terms[k], 0.0)
                    return total

                found = lax.fori_loop(
                    0, TAPS // GROUP // QUAD, step, jnp.zeros((PART, LANES), F32)
                )
                dhk[rows, part] = (found * hv[rows, part].astype(F32)).astype(BF16)
                dhv[rows, part] = (found * hk[rows, part].astype(F32)).astype(BF16)

        correlate(0)
        hear(2)
        filter_out(0)
        give_grads(0)
        service(1)
        correlate(1)
        filter_out(1)
        service(2)
        correlate(2)
        filter_out(2)
        correlate(3)
        filter_out(3)
        attend(1)
        service(3)
        attend(2)
        give_grads(1)
        attend(3)
        filter_sum(0)
        give_grads(2)
        give_grads(3)

        @pl.loop(0, columns)
        def _(column):
            part = lanes(column)
            slope = squares[...] * weighted[:, part] - gated[:, part] * crossed[...]
            dhq[:, part] = (slope * mixed[:, part]).astype(BF16)

        stores[3].start()
        sig_copy.wait_recv()
        sig[ROWS:, :] = sig_in[...].astype(F32)
        spread(0)
        spread(1)
        spread(2)
        spread(3)
        stores[4].start()
        stores[5].start()
        take_grads(0)
        filter_whole(0)
        take_grads(1)
        take_grads(2)
        take_grads(3)
        for place in range(3):
            stores[place].start()

        halo_copy(0).wait_send()
        halo_copy(1).wait_send()
        sig_copy.wait_send()
        for step in range(1, m):
            sum_copy(step).wait_send()
        for head in range(heads):
            for made in (
                give_back, give_queries, give_on, near_copy, far_copy, gs_copy, dq_copy, up_copy,
                down_copy,
            ):
                made(head).wait_send()
        for chunk in range(chunks):
            wait_bytes(fa_in, f_send, 0, chunk, crew - 1)
            wait_bytes(fb, f_send, 1, chunk, pairs - 1)
        for chunk in range(chunks):
            filter_done(chunk)
        stores[6].start()
        for chunk in range(chunks):
            wait_bytes(fd, f_send, 2, chunk, crew - 1)
        for store in stores:
            store.wait()

    vmem = pltpu.VMEM
    dma = pltpu.SemaphoreType.DMA
    square = (ROWS, LANES)
    wide = vmem((ROWS, width), BF16)
    scratch = [
        wide, wide, wide, wide, wide, wide,
        wide, wide, wide, wide,
        vmem((width, TAPS), F32),
        vmem((1, width), F32),
        vmem((n, ROWS), jnp.int32),
        vmem((ROWS, LANES), F32),
        vmem((3 * ROWS, LANES), F32),
        vmem((keys, ROWS), F32),
        vmem((TAPS, width), F32),
        vmem((2 * ROWS, width), F32),
        vmem((2, ROWS, width // 2), BF16),
        vmem((2, ROWS, width // 2), BF16),
        vmem((GROUP, 2 * ROWS, width), F32),
        vmem((ROWS, width), F32),
        vmem((ROWS, width), F32),
        vmem((ROWS, width), F32),
        vmem(square, F32),
        vmem(square, F32),
        vmem((8, ROWS), F32),
        vmem((max(1, m - 1), 8, ROWS), F32),
        vmem((2 * ROWS, width), F32),
        wide,
        wide,
        vmem((GROUP, 2 * ROWS - GROUP, LANES), F32),
        vmem((TAPS, width), F32),
        vmem((chunks, crew, sides * crew_taps, LANES), BF16),
        vmem((chunks, crew - 1, sides * crew_taps, LANES), BF16),
        vmem((chunks, pairs, sides * crew_taps, LANES), BF16),
        vmem((chunks, crew, sides * crew_taps, LANES), BF16),
        vmem((heads, SPAN + 1, 2, ROWS, HEAD_DIM), BF16),
        vmem((heads, 2, ROWS, HEAD_DIM), BF16),
        vmem((heads, 2, ROWS, HEAD_DIM), BF16),
        vmem((heads, ROWS, HEAD_DIM), BF16),
        vmem((heads, ROWS, HEAD_DIM), BF16),
        vmem((heads, 2, keys, HEAD_DIM), F32),
        vmem((heads, 2, 2, ROWS, HEAD_DIM), BF16),
        vmem((heads, 2, 2, ROWS, HEAD_DIM), BF16),
        vmem((heads, 2, ROWS, HEAD_DIM), BF16),
        vmem((heads, 2, ROWS, HEAD_DIM), BF16),
        vmem((heads, 2, ROWS, HEAD_DIM), BF16),
        vmem((heads, 2, ROWS, HEAD_DIM), BF16),
        dma((7 + 4 * heads,)),
        dma((3,)),
        dma((3,)),
        dma((max(1, m - 1),)),
        dma((max(1, m - 1),)),
        dma((heads, 5)),
        dma((heads, 5)),
        dma((heads, 4)),
        dma((heads, 4)),
        dma((3, chunks)),
        dma((3, chunks)),
        pltpu.SemaphoreType.REGULAR((3,)),
        dma((7,)),
    ]
    return kernel, scratch, (chunks, crew, sides * crew_taps, LANES)


def write_out(*refs):
    sources, results, held, (dfilter, sems) = refs[:7], refs[7:14], refs[14:21], refs[21:]
    loads = [
        pltpu.make_async_copy(src, mid, sems.at[0, place])
        for place, (src, mid) in enumerate(zip(sources, held))
    ]
    stores = [
        pltpu.make_async_copy(mid, dst, sems.at[1, place])
        for place, (mid, dst) in enumerate(zip((*held[:6], dfilter), results))
    ]
    for load in reversed(loads):
        load.start()
    loads[6].wait()
    fd = held[6]
    chunks, crew, rows, _ = fd.shape
    taps = TAPS // crew
    sides = rows // taps
    for chunk in range(chunks):
        for side in range(sides):
            tap_rows = fd[chunk, :, side * taps : (side + 1) * taps].astype(F32)
            begin = (sides * chunk + side) * LANES
            dfilter[begin : begin + LANES, :] = tap_rows.reshape(TAPS, LANES).T
    stores[6].start()
    for load, store in zip(loads[:6], stores[:6]):
        load.wait()
        store.start()
    for store in stores:
        store.wait()


def build(mesh, line):
    n, m = mesh.shape["ctx"], mesh.shape["mp"]

    def body(aq, ak, av, ao, hq, hk, hv, ho, taps, gain, seg):
        rows, width = aq.shape
        kernel, scratch, rows_shape = make_kernel(n, m, width, line)
        wide = jax.ShapeDtypeStruct((rows, width), BF16)
        shapes = (wide,) * 6 + (jax.ShapeDtypeStruct((width, TAPS), F32),)
        found_shapes = (wide,) * 6 + (jax.ShapeDtypeStruct(rows_shape, BF16),)
        far = pl.BlockSpec(memory_space=pltpu.HBM)
        found = pl.pallas_call(
            kernel,
            out_shape=found_shapes,
            in_specs=[far] * 11,
            out_specs=(far,) * 7,
            scratch_shapes=scratch,
            compiler_params=pltpu.CompilerParams(
                collective_id=0, has_side_effects=True, vmem_limit_bytes=60 * 2**20
            ),
        )(aq, ak, av, ao, hq, hk, hv, ho, taps, gain.reshape(1, width), seg.reshape(n, rows))
        return pl.pallas_call(
            write_out,
            out_shape=shapes,
            in_specs=[far] * 7,
            out_specs=(far,) * 7,
            scratch_shapes=[pltpu.VMEM(one.shape, one.dtype) for one in found_shapes]
            + [pltpu.VMEM((width, TAPS), F32), pltpu.SemaphoreType.DMA((2, 7))],
            compiler_params=pltpu.CompilerParams(vmem_limit_bytes=60 * 2**20),
        )(*found)

    wide = P("ctx", "mp")
    return jax.shard_map(
        body,
        mesh=mesh,
        in_specs=(wide,) * 8 + (P("mp", None), P("mp"), P()),
        out_specs=(wide,) * 6 + (P("mp", None),),
        check_vma=False,
    )


def solution(mesh):
    return build(mesh, LINE)
```
